32 devices in a mesh: span: 2 (over y), tm: 16 (over z, x, core).
Axes of the slice: x: 2, y: 2, z: 4, core: 2. Of those that a mesh axis runs over, the one named last changes fastest.
Arguments:
- traces: bfloat16 [1024, 32768], P(None, ('span', 'tm')), parts along dimension 1, may hold values from -6 to 6
- templates: bfloat16 [256, 16, 512], P('tm'), may hold values from -6 to 6
- blocks: int32 [16, 4], replicated, may hold values from 0 to 7, all different within a row
Outputs:
- detection: float32 [16, 32768], P(None, ('span', 'tm')), parts along dimension 1
The draws below stay inside these ranges and needn't reach their ends.
There are 2 independent parts, one for each index of `span`. The reference program is written for one: setup_inputs(seed, part) draws one part's arguments, and reference() takes and returns one part's arrays. A program takes and returns all parts, laid end to end along the dimension named above; an argument that names none is the same for every part. Nothing has to cross between parts.
Inputs may be any that keep to these rules, and one draw needn't show every extreme that they name: Each row lists 4 different channel blocks.
All inputs are finite; a program needn't handle non-finite values.
Results may differ from the reference program's by a relative error of at most 0.0003.
Values may be sent and summed in bfloat16 or wider, within the bound.
A program may use at most 128 MiB of HBM per device.

```python
import math
import jax
import jax.numpy as jnp
from jax import lax

C = 1024
MAXB = 4
K = 256
J = 16
NB = 8
R = 512
NT = 16384
N_TM = 16


def steps_of(key, dims, pieces, least, top_value):
    loudness = 1.0
    for axis_at, parts in pieces:
        steps = jax.random.uniform(jax.random.fold_in(jax.random.fold_in(key, 6), axis_at), (parts,), jnp.float32, least / len(pieces), top_value / len(pieces))
        loudness = loudness * jnp.repeat(jnp.exp(steps), dims[axis_at] // parts).reshape((-1,) + (1,) * (len(dims) - 1 - axis_at))
    return loudness


def distinct(own_key, rows, count, top, lift):
    sequence = jax.random.permutation(jax.random.fold_in(own_key, 1), count)
    pull = sequence
    for power in range(3):
        pull = pull * pull // count
    pull = pull * lift // count
    lots = jax.random.randint(jax.random.fold_in(own_key, 2), (rows, count), 0, 4096) + pull
    holders = jax.random.permutation(jax.random.fold_in(own_key, 3), rows)[jnp.arange(count) % rows]
    lots = jnp.where(jnp.arange(rows)[:, None] == holders[None, :], 1 << 14, lots)
    priority = lots * count + jnp.arange(count)
    return lax.top_k(priority.astype(jnp.int32), top)[1].astype(jnp.int32)


def scatter_about(rng, dims, spread, reach, shards=(), kind=jnp.bfloat16):
    array = spread * jax.random.normal(rng, dims, jnp.float32)
    if shards:
        array = array * steps_of(rng, dims, shards, -0.22, 0.18)
    return jnp.clip(array, -reach, reach).astype(kind)


def setup_inputs(seed: int = 0, part: int = 0) -> dict:
    streams_of = jax.random.split(jax.random.key(seed), 4)
    part_splits = jax.random.split(jax.random.fold_in(streams_of[3], part), 4)
    return {
        "traces": scatter_about(part_splits[0], (C, NT), 1.0, 6.0, ((1, 16),)),
        "templates": scatter_about(streams_of[1], (K, J, R), 1.0, 6.0, ((0, 16),)),
        "blocks": distinct(streams_of[2], J, NB, MAXB, 0),
    }


epsilon = 1e-06

def sheared_sum(product, lag_count):
    members, tap_count, span_width = product.shape
    flattened = product.reshape(members, tap_count * span_width)
    flattened = jnp.pad(flattened, ((0, 0), (0, tap_count)))
    return flattened.reshape(members, tap_count, span_width + 1)[:, :, :lag_count].sum(axis=1)

def reference(traces, templates, blocks):
    channels, total = traces.shape
    tap_count, members, row_count = templates.shape
    listed = blocks.shape[1]
    block_rows = row_count // listed
    nblocks = channels // block_rows
    lag_count = total // N_TM
    span_width = lag_count + tap_count
    padded = jnp.pad(traces, ((0, 0), (0, tap_count)))
    starts = jnp.arange(N_TM, dtype=jnp.int32) * lag_count
    selector = (blocks[:, :, None] == jnp.arange(nblocks, dtype=jnp.int32)[None, None, :]).astype(jnp.float32)
    counting = selector.sum(axis=1)
    weights_wide = templates.astype(jnp.float32)
    norm_sums = lax.optimization_barrier(jnp.sum(jnp.square(weights_wide), axis=(0, 2)))
    scale_factor = math.sqrt(tap_count * row_count)

    def one_block(start):
        extended = lax.dynamic_slice(padded, (jnp.int32(0), start), (channels, span_width))
        squares = jnp.square(extended.astype(jnp.float32)).reshape(nblocks, block_rows, span_width).sum(axis=1)
        running = jnp.concatenate([jnp.zeros((nblocks, 1), jnp.float32), jnp.cumsum(squares, axis=1)], axis=1)
        window = running[:, tap_count:tap_count + lag_count] - running[:, :lag_count]
        energy = jnp.dot(counting, window, precision=lax.Precision.HIGHEST)
        chosen = extended.reshape(nblocks, block_rows, span_width)[blocks]
        chosen = chosen.reshape(members, row_count, span_width).astype(jnp.float32)
        product = jnp.einsum('kqr,qrl->qkl', weights_wide, chosen, precision=lax.Precision.HIGHEST)
        correlation = sheared_sum(product, lag_count)
        denominator = energy * norm_sums[:, None] + epsilon
        return correlation * lax.rsqrt(denominator) * scale_factor
    stacked = lax.map(one_block, starts)
    return jnp.transpose(stacked, (1, 0, 2)).reshape(members, total)
```

```python
import functools
import math

import jax
import jax.numpy as jnp
from jax import lax
from jax.experimental import pallas as pl
from jax.experimental.pallas import tpu as pltpu
from jax.sharding import PartitionSpec as P

epsilon = 1e-06
MESH = pl.DeviceIdType.MESH


template_groups = 4


def from_behind(block, axis, distance):
    devices = range(lax.axis_size(axis))
    route = [(i - distance, i) for i in devices if i - distance in devices]
    return lax.ppermute(block, axis, route)


def tap_total(product, lag_count):
    members, tap_count, span_width = product.shape
    flattened = product.reshape(members, tap_count * span_width)
    flattened = jnp.pad(flattened, ((0, 0), (0, tap_count)))
    return flattened.reshape(members, tap_count, span_width + 1)[:, :, :lag_count].sum(axis=1)


def plain(traces, templates, blocks):
    channels, lag_count = traces.shape
    local_taps, members, row_count = templates.shape
    listed = blocks.shape[1]
    block_rows = row_count // listed
    nblocks = channels // block_rows
    tap_count = local_taps * lax.axis_size("tm")
    incoming = from_behind(traces[:, :tap_count], "tm", -1)
    source = jnp.concatenate([traces, incoming], axis=1)
    span_width = source.shape[1]
    squares = (
        jnp.square(source.astype(jnp.float32)).reshape(nblocks, block_rows, span_width).sum(axis=1)
    )
    running = jnp.concatenate(
        [jnp.zeros((nblocks, 1), jnp.float32), jnp.cumsum(squares, axis=1)], axis=1
    )
    window = running[:, tap_count : tap_count + lag_count] - running[:, :lag_count]
    selector = (blocks[:, :, None] == jnp.arange(nblocks, dtype=jnp.int32)[None, None, :]).astype(
        jnp.float32
    )
    counting = selector.sum(axis=1)
    scale_factor = math.sqrt(tap_count * row_count)
    group_size = members // template_groups
    gathered = lax.all_gather(templates, "tm", axis=0, tiled=True)
    pieces = []
    norm_pieces = []
    for group_index in range(template_groups):
        offset = group_index * group_size
        weights = gathered[:, offset : offset + group_size]
        chosen = source.reshape(nblocks, block_rows, span_width)[
            blocks[offset : offset + group_size]
        ]
        chosen = chosen.reshape(group_size, row_count, span_width)
        product = jnp.einsum("kqr,qrl->qkl", weights, chosen, preferred_element_type=jnp.float32)
        pieces.append(tap_total(product, lag_count))
        norm_pieces.append(jnp.sum(jnp.square(weights.astype(jnp.float32)), axis=(0, 2)))
    correlation = jnp.concatenate(pieces, axis=0)
    norm_sums = jnp.concatenate(norm_pieces, axis=0)
    energy = jnp.dot(counting, window, precision=lax.Precision.HIGHEST)
    denominator = energy * norm_sums[:, None] + epsilon
    return correlation * lax.rsqrt(denominator) * scale_factor


def only(condition, action):
    @pl.when(condition)
    def _():
        action()


UP, DOWN, ACROSS, PLANE = range(4)


def kernel(
    tm,
    blocks_s, blocks_v, traces, templates, out,
    X, W, S, CP, CC, CN, RC, RN, RP, E, EN,
    x_sem, slab_sem, send_sem, recv_sem, tail_send, tail_recv,
):
    nblocks, depth, lags = traces.shape
    local_taps, members, rows = templates.shape
    listed = blocks_s.shape[1]
    taps = local_taps * tm
    half = members // 2
    pair_taps = 2 * local_taps
    line = tm // 4
    chips = tm // 2
    shared = (3 * half // 4) // 2
    scale = math.sqrt(taps * rows)

    me = lax.axis_index("tm")
    plane = lax.axis_index("span")
    core = lax.rem(me, 2)
    chip = me // 2
    x = lax.rem(chip, 2)
    z = chip // 2

    def device(z_, x_, c_):
        return {"tm": (z_ * 2 + x_) * 2 + c_}

    sibling = device(z, x, 1 - core)
    targets = {
        UP: device(z + 1, x, core),
        DOWN: device(z - 1, x, core),
        ACROSS: device(z, 1 - x, core),
        PLANE: {"span": 1 - plane},
    }
    has_up, has_down = z + 1 < line, z > 0
    has_next, has_prev = chip + 1 < chips, chip > 0

    barrier = pltpu.get_barrier_semaphore()

    def greet(target):
        pl.semaphore_signal(barrier, inc=1, device_id=target, device_id_type=MESH)

    greet(sibling)
    greet(targets[ACROSS])
    greet(targets[PLANE])
    only(has_up, lambda: greet(targets[UP]))
    only(has_down, lambda: greet(targets[DOWN]))

    @pl.when(jnp.logical_and(has_next, core == 1))
    def _():
        greet({"tm": 2 * chip + 2})
        greet({"tm": 2 * chip + 3})

    own_traces = pltpu.make_async_copy(traces, X.at[core], x_sem.at[0])
    own_traces.start()
    S[...] = jnp.swapaxes(templates[...], 0, 1)
    slab_rows = pl.ds(pl.multiple_of(me * local_taps, local_taps), local_taps)
    own_slab = pltpu.make_async_copy(
        S.at[pl.ds(core * half, half)], W.at[:, slab_rows, :], slab_sem.at[0]
    )
    own_slab.start()

    greetings = 3 + has_up.astype(jnp.int32) + has_down.astype(jnp.int32) + has_prev.astype(jnp.int32)
    pl.semaphore_wait(barrier, greetings)

    def remote(src, dst, send, recv, target):
        return pltpu.make_async_remote_copy(
            src_ref=src, dst_ref=dst, send_sem=send, recv_sem=recv,
            device_id=target, device_id_type=MESH,
        )

    other_slab = remote(
        S.at[pl.ds((1 - core) * half, half)], W.at[:, slab_rows, :],
        slab_sem.at[1], slab_sem.at[2], sibling,
    )
    other_slab.start()
    other_traces = remote(traces, X.at[core], x_sem.at[1], x_sem.at[2], sibling)

    started = []

    def move(way, j, p):
        part = W.at[j, pl.ds(pl.multiple_of(p * pair_taps, pair_taps), pair_taps), :]
        return remote(part, part, send_sem.at[way, j, p], recv_sem.at[j, p], targets[way])

    def send(way, j, p, allowed):
        started.append((way, j, p, allowed))
        only(allowed, lambda: move(way, j, p).start())

    def arrived(j, p, allowed):
        only(allowed, lambda: move(ACROSS, j, p).wait_recv())

    own_slab.wait()
    other_slab.wait_recv()

    mine = [plane * shared + i for i in range(shared)]
    theirs = [(1 - plane) * shared + i for i in range(shared)]
    both = list(range(2 * shared, half))
    flows = [(j, True) for j in mine] + [(j, False) for j in both]
    always = z >= 0

    def stage(flow, k):
        j, passed_on = flow
        here = lambda d: (z + d) * 2 + x
        there = lambda d: (z + d) * 2 + 1 - x
        if k == 0:
            send(UP, j, here(0), has_up)
            send(DOWN, j, here(0), has_down)
            send(ACROSS, j, here(0), always)
            return
        if k < line:
            below, above = z >= k, z + k < line
            arrived(j, here(-k), below)
            send(UP, j, here(-k), jnp.logical_and(below, has_up))
            send(ACROSS, j, here(-k), below)
            if passed_on:
                send(PLANE, j, here(-k), below)
            arrived(j, here(k), above)
            send(DOWN, j, here(k), jnp.logical_and(above, has_down))
            send(ACROSS, j, here(k), above)
            if passed_on:
                send(PLANE, j, here(k), above)
        d = k - 1
        if d == 0:
            arrived(j, there(0), always)
            if passed_on:
                send(PLANE, j, there(0), always)
        else:
            below, above = z >= d, z + d < line
            arrived(j, there(-d), below)
            if passed_on:
                send(PLANE, j, there(-d), below)
            arrived(j, there(d), above)
            if passed_on:
                send(PLANE, j, there(d), above)

    def passed(j):
        for d in range(1, chips):
            arrived(j, lax.rem(chip + d, chips), always)

    def correlate(j):
        weights = W[j]
        width = lags + taps
        partial = []
        names = [blocks_s[core * half + j, m] for m in range(listed)]
        half_taps = taps // 2
        for h in range(2):
            chosen = jnp.concatenate([X[h, b] for b in names], axis=0)
            product = jnp.dot(weights, chosen, preferred_element_type=jnp.float32)
            total = None
            for row in range(0, half_taps, 8):
                near = product[row : row + 8]
                far = product[row + half_taps : row + half_taps + 8]
                gap = jnp.zeros((8, half_taps), jnp.float32)
                joined = jnp.concatenate([far, gap], axis=1) + jnp.concatenate([gap, near], axis=1)
                joined = jnp.concatenate([gap, joined], axis=1)
                if row:
                    joined = pltpu.roll(joined, width - row, 1)
                total = joined if total is None else total + joined
            partial.append(total)
        gap = jnp.zeros((8, lags), jnp.float32)
        sheared = jnp.concatenate([partial[0], gap], axis=1) + jnp.concatenate(
            [gap, partial[1]], axis=1
        )
        row_index = lax.broadcasted_iota(jnp.int32, sheared.shape, 0)
        for bit in (1, 2, 4):
            moved = pltpu.roll(sheared, sheared.shape[1] - bit, 1)
            sheared = jnp.where(lax.rem(row_index // bit, 2) == 1, moved, sheared)
        line_sum = jnp.sum(sheared, axis=0, keepdims=True)
        CP[pl.ds(j, 1), :] = line_sum[:, :taps]
        CC[0, pl.ds(j, 1), :] = line_sum[:, taps : taps + lags]
        CC[1, pl.ds(j, 1), :] = line_sum[:, taps + lags :]
        wide = weights.astype(jnp.float32)
        norm = jnp.sum(jnp.sum(wide * wide, axis=0, keepdims=True), axis=1, keepdims=True)
        CN[pl.ds(j, 1), :] = jnp.broadcast_to(norm, (1, CN.shape[1]))

    edge_send = remote(
        E.at[:, pl.ds(0, taps)], E.at[:, pl.ds(lags, taps)],
        tail_send.at[0], tail_recv.at[0], {"tm": me - 1},
    )

    def energies():
        own_traces.wait()
        for b in range(nblocks):
            part = X[core, b].astype(jnp.float32)
            E[pl.ds(b, 1), pl.ds(0, lags)] = jnp.sum(part * part, axis=0, keepdims=True)
        only(me > 0, edge_send.start)

        @pl.when(me + 1 == tm)
        def _():
            E[:, pl.ds(lags, taps)] = jnp.zeros((nblocks, taps), jnp.float32)

    def windows():
        only(me + 1 < tm, edge_send.wait_recv)
        window = E[...]
        reach = 1
        while reach < taps:
            window = window + pltpu.roll(window, window.shape[1] - reach, 1)
            reach *= 2
        window = window[:, :lags]
        table = blocks_v[...]
        energy = jnp.zeros((members, lags), jnp.float32)
        for b in range(nblocks):
            count = jnp.sum((table == b).astype(jnp.float32), axis=1, keepdims=True)
            energy = energy + count * window[b : b + 1]
        EN[...] = energy

    order = {}
    steps = len(flows) + line
    for s in range(steps + 1):
        for i, flow in enumerate(flows):
            if 0 <= s - i <= line:
                stage(flow, s - i)
        if s == 0:
            other_traces.start()
            energies()
        if s == 1:
            windows()
        if s == line - 1:
            other_traces.wait_recv()
        i = s - line
        if 0 <= i < len(flows):
            correlate(flows[i][0])
        if s == steps - 2 and shared:
            passed(theirs[0])
            correlate(theirs[0])
    for j in theirs[1:]:
        passed(j)
        correlate(j)

    mate = remote(CC.at[1 - core], RC, tail_send.at[1], tail_recv.at[1], sibling)
    norms = remote(CN, RN, tail_send.at[2], tail_recv.at[2], sibling)
    before = remote(
        CP, RP.at[core], tail_send.at[3], tail_recv.at[3 + core], {"tm": 2 * chip - 1}
    )
    mate.start()
    norms.start()
    only(has_prev, before.start)
    mate.wait_recv()
    norms.wait_recv()

    mine_rows = pl.ds(pl.multiple_of(core * half, half), half)
    mate_rows = pl.ds(pl.multiple_of((1 - core) * half, half), half)

    takes = jnp.logical_and(has_next, core == 1)

    @pl.when(takes)
    def _():
        for c in range(2):
            remote(CP, RP.at[c], tail_send.at[3], tail_recv.at[3 + c], sibling).wait_recv()

    def finish(value, rows_, norm, tail):
        denominator = EN[rows_, :] * norm[:, :1] + epsilon
        factor = lax.rsqrt(denominator) * scale
        out[rows_, :] = value * factor

        @pl.when(takes)
        def _():
            last = pl.ds(lags - taps, taps)
            out[rows_, last] = (value[:, lags - taps :] + tail()) * factor[:, lags - taps :]

    finish(CC[core], mine_rows, CN[...], lambda: RP[core])
    finish(RC[...], mate_rows, RN[...], lambda: RP[1 - core])

    other_slab.wait_send()
    other_traces.wait_send()
    mate.wait_send()
    norms.wait_send()
    only(has_prev, before.wait_send)
    only(me > 0, edge_send.wait_send)
    for way, j, p, allowed in started:
        only(allowed, move(way, j, p).wait_send)


def fused(traces, templates, blocks):
    channels, lags = traces.shape
    local_taps, members, rows = templates.shape
    tm = lax.axis_size("tm")
    taps = local_taps * tm
    half = members // 2
    depth = rows // blocks.shape[1]
    nblocks = channels // depth
    chips = tm // 2
    vmem = pl.BlockSpec(memory_space=pltpu.VMEM)
    f32 = jnp.float32
    return pl.pallas_call(
        functools.partial(kernel, tm),
        out_shape=jax.ShapeDtypeStruct((members, lags), f32),
        in_specs=[
            pl.BlockSpec(memory_space=pltpu.SMEM),
            vmem,
            pl.BlockSpec(memory_space=pl.ANY),
            vmem,
        ],
        out_specs=vmem,
        scratch_shapes=[
            pltpu.VMEM((2, nblocks, depth, lags), traces.dtype),
            pltpu.VMEM((half, taps, rows), templates.dtype),
            pltpu.VMEM((members, local_taps, rows), templates.dtype),
            pltpu.VMEM((half, taps), f32),
            pltpu.VMEM((2, half, lags), f32),
            pltpu.VMEM((half, 128), f32),
            pltpu.VMEM((half, lags), f32),
            pltpu.VMEM((half, 128), f32),
            pltpu.VMEM((2, half, taps), f32),
            pltpu.VMEM((nblocks, lags + taps), f32),
            pltpu.VMEM((members, lags), f32),
            pltpu.SemaphoreType.DMA((3,)),
            pltpu.SemaphoreType.DMA((3,)),
            pltpu.SemaphoreType.DMA((4, half, chips)),
            pltpu.SemaphoreType.DMA((half, chips)),
            pltpu.SemaphoreType.DMA((4,)),
            pltpu.SemaphoreType.DMA((5,)),
        ],
        compiler_params=pltpu.CompilerParams(
            collective_id=0, has_side_effects=True, vmem_limit_bytes=48 * 2**20
        ),
    )(blocks, blocks, traces.reshape(nblocks, depth, lags), templates)


def per_device(traces, templates, blocks):
    channels, lags = traces.shape
    local_taps, members, rows = templates.shape
    tm = lax.axis_size("tm")
    taps = local_taps * tm
    fits = (
        lax.axis_size("span") == 2
        and tm % 4 == 0
        and local_taps % 16 == 0
        and members == 16
        and taps == 256
        and lags % 128 == 0
        and rows % (128 * blocks.shape[1]) == 0
    )
    return (fused if fits else plain)(traces, templates, blocks)


def solution(mesh):
    return jax.shard_map(
        per_device,
        mesh=mesh,
        in_specs=(P(None, ("span", "tm")), P("tm", None, None), P()),
        out_specs=P(None, ("span", "tm")),
        check_vma=False,
    )
```

```python
import functools
import math

import jax
import jax.numpy as jnp
from jax import lax
from jax.experimental import pallas as pl
from jax.experimental.pallas import tpu as pltpu
from jax.sharding import PartitionSpec as P

epsilon = 1e-06
MESH = pl.DeviceIdType.MESH


template_groups = 4


def from_behind(block, axis, distance):
    devices = range(lax.axis_size(axis))
    route = [(i - distance, i) for i in devices if i - distance in devices]
    return lax.ppermute(block, axis, route)


def tap_total(product, lag_count):
    members, tap_count, span_width = product.shape
    flattened = product.reshape(members, tap_count * span_width)
    flattened = jnp.pad(flattened, ((0, 0), (0, tap_count)))
    return flattened.reshape(members, tap_count, span_width + 1)[:, :, :lag_count].sum(axis=1)


def plain(traces, templates, blocks):
    channels, lag_count = traces.shape
    local_taps, members, row_count = templates.shape
    listed = blocks.shape[1]
    block_rows = row_count // listed
    nblocks = channels // block_rows
    tap_count = local_taps * lax.axis_size("tm")
    incoming = from_behind(traces[:, :tap_count], "tm", -1)
    source = jnp.concatenate([traces, incoming], axis=1)
    span_width = source.shape[1]
    squares = (
        jnp.square(source.astype(jnp.float32)).reshape(nblocks, block_rows, span_width).sum(axis=1)
    )
    running = jnp.concatenate(
        [jnp.zeros((nblocks, 1), jnp.float32), jnp.cumsum(squares, axis=1)], axis=1
    )
    window = running[:, tap_count : tap_count + lag_count] - running[:, :lag_count]
    selector = (blocks[:, :, None] == jnp.arange(nblocks, dtype=jnp.int32)[None, None, :]).astype(
        jnp.float32
    )
    counting = selector.sum(axis=1)
    scale_factor = math.sqrt(tap_count * row_count)
    group_size = members // template_groups
    gathered = lax.all_gather(templates, "tm", axis=0, tiled=True)
    pieces = []
    norm_pieces = []
    for group_index in range(template_groups):
        offset = group_index * group_size
        weights = gathered[:, offset : offset + group_size]
        chosen = source.reshape(nblocks, block_rows, span_width)[
            blocks[offset : offset + group_size]
        ]
        chosen = chosen.reshape(group_size, row_count, span_width)
        product = jnp.einsum("kqr,qrl->qkl", weights, chosen, preferred_element_type=jnp.float32)
        pieces.append(tap_total(product, lag_count))
        norm_pieces.append(jnp.sum(jnp.square(weights.astype(jnp.float32)), axis=(0, 2)))
    correlation = jnp.concatenate(pieces, axis=0)
    norm_sums = jnp.concatenate(norm_pieces, axis=0)
    energy = jnp.dot(counting, window, precision=lax.Precision.HIGHEST)
    denominator = energy * norm_sums[:, None] + epsilon
    return correlation * lax.rsqrt(denominator) * scale_factor


def only(condition, action):
    @pl.when(condition)
    def _():
        action()


UP, DOWN, ACROSS, PLANE = range(4)


def kernel(
    tm,
    listing, traces, templates, out,
    T, X, W, S, CP, CC, CN, RC, RN, RP, E, WIN, EN,
    t_sem, x_sem, slab_sem, send_sem, recv_sem, tail_send, tail_recv,
):
    nblocks, depth, lags = traces.shape
    local_taps, members, rows = templates.shape
    listed = listing.shape[0]
    taps = local_taps * tm
    half = members // 2
    pair_taps = 2 * local_taps
    line = tm // 4
    chips = tm // 2
    shared = (3 * half // 4) // 2
    scale = math.sqrt(taps * rows)

    me = lax.axis_index("tm")
    plane = lax.axis_index("span")
    core = lax.rem(me, 2)
    chip = me // 2
    x = lax.rem(chip, 2)
    z = chip // 2

    def device(z_, x_, c_):
        return {"tm": (z_ * 2 + x_) * 2 + c_}

    sibling = device(z, x, 1 - core)
    targets = {
        UP: device(z + 1, x, core),
        DOWN: device(z - 1, x, core),
        ACROSS: device(z, 1 - x, core),
        PLANE: {"span": 1 - plane},
    }
    has_up, has_down = z + 1 < line, z > 0
    has_next, has_prev = chip + 1 < chips, chip > 0

    own_templates = pltpu.make_async_copy(templates, T, t_sem)
    own_templates.start()

    barrier = pltpu.get_barrier_semaphore()

    def greet(target):
        pl.semaphore_signal(barrier, inc=1, device_id=target, device_id_type=MESH)

    greet(sibling)
    greet(targets[ACROSS])
    greet(targets[PLANE])
    only(has_up, lambda: greet(targets[UP]))
    only(has_down, lambda: greet(targets[DOWN]))

    @pl.when(jnp.logical_and(has_next, core == 1))
    def _():
        greet({"tm": 2 * chip + 2})
        greet({"tm": 2 * chip + 3})

    own_traces = pltpu.make_async_copy(traces, X.at[core], x_sem.at[0])
    own_traces.start()
    own_templates.wait()
    S[...] = jnp.swapaxes(T[...], 0, 1)
    slab_rows = pl.ds(pl.multiple_of(me * local_taps, local_taps), local_taps)
    own_slab = pltpu.make_async_copy(
        S.at[pl.ds(core * half, half)], W.at[:, slab_rows, :], slab_sem.at[0]
    )
    own_slab.start()

    greetings = 3 + has_up.astype(jnp.int32) + has_down.astype(jnp.int32) + has_prev.astype(jnp.int32)
    pl.semaphore_wait(barrier, greetings)

    def remote(src, dst, send, recv, target):
        return pltpu.make_async_remote_copy(
            src_ref=src, dst_ref=dst, send_sem=send, recv_sem=recv,
            device_id=target, device_id_type=MESH,
        )

    other_slab = remote(
        S.at[pl.ds((1 - core) * half, half)], W.at[:, slab_rows, :],
        slab_sem.at[1], slab_sem.at[2], sibling,
    )
    other_slab.start()
    other_traces = remote(traces, X.at[core], x_sem.at[1], x_sem.at[2], sibling)

    started = []

    def move(way, j, p):
        part = W.at[j, pl.ds(pl.multiple_of(p * pair_taps, pair_taps), pair_taps), :]
        return remote(part, part, send_sem.at[way, j, p], recv_sem.at[j, p], targets[way])

    def send(way, j, p, allowed):
        started.append((way, j, p, allowed))
        only(allowed, lambda: move(way, j, p).start())

    def arrived(j, p, allowed):
        only(allowed, lambda: move(ACROSS, j, p).wait_recv())

    own_slab.wait()
    other_slab.wait_recv()

    mine = [plane * shared + i for i in range(shared)]
    theirs = [(1 - plane) * shared + i for i in range(shared)]
    both = list(range(2 * shared, half))
    flows = [(j, True) for j in mine] + [(j, False) for j in both]
    always = z >= 0

    def stage(flow, k):
        j, passed_on = flow
        here = lambda d: (z + d) * 2 + x
        there = lambda d: (z + d) * 2 + 1 - x
        if k == 0:
            send(UP, j, here(0), has_up)
            send(DOWN, j, here(0), has_down)
            send(ACROSS, j, here(0), always)
            return
        if k < line:
            below, above = z >= k, z + k < line
            arrived(j, here(-k), below)
            send(UP, j, here(-k), jnp.logical_and(below, has_up))
            send(ACROSS, j, here(-k), below)
            if passed_on:
                send(PLANE, j, here(-k), below)
            arrived(j, here(k), above)
            send(DOWN, j, here(k), jnp.logical_and(above, has_down))
            send(ACROSS, j, here(k), above)
            if passed_on:
                send(PLANE, j, here(k), above)
        d = k - 1
        if d == 0:
            arrived(j, there(0), always)
            if passed_on:
                send(PLANE, j, there(0), always)
        else:
            below, above = z >= d, z + d < line
            arrived(j, there(-d), below)
            if passed_on:
                send(PLANE, j, there(-d), below)
            arrived(j, there(d), above)
            if passed_on:
                send(PLANE, j, there(d), above)

    def passed(j):
        for d in range(1, chips):
            arrived(j, lax.rem(chip + d, chips), always)

    def correlate(j):
        weights = W[j]
        width = lags + taps
        partial = []
        names = [listing[m, core * half + j] for m in range(listed)]
        half_taps = taps // 2
        for h in range(2):
            chosen = jnp.concatenate([X[h, b] for b in names], axis=0)
            product = jnp.dot(weights, chosen, preferred_element_type=jnp.float32)
            total = None
            for row in range(0, half_taps, 8):
                near = product[row : row + 8]
                far = product[row + half_taps : row + half_taps + 8]
                gap = jnp.zeros((8, half_taps), jnp.float32)
                joined = jnp.concatenate([far, gap], axis=1) + jnp.concatenate([gap, near], axis=1)
                joined = jnp.concatenate([gap, joined], axis=1)
                if row:
                    joined = pltpu.roll(joined, width - row, 1)
                total = joined if total is None else total + joined
            partial.append(total)
        gap = jnp.zeros((8, lags), jnp.float32)
        sheared = jnp.concatenate([partial[0], gap], axis=1) + jnp.concatenate(
            [gap, partial[1]], axis=1
        )
        row_index = lax.broadcasted_iota(jnp.int32, sheared.shape, 0)
        for bit in (1, 2, 4):
            moved = pltpu.roll(sheared, sheared.shape[1] - bit, 1)
            sheared = jnp.where(lax.rem(row_index // bit, 2) == 1, moved, sheared)
        line_sum = jnp.sum(sheared, axis=0, keepdims=True)
        CP[pl.ds(j, 1), :] = line_sum[:, :taps]
        CC[0, pl.ds(j, 1), :] = line_sum[:, taps : taps + lags]
        CC[1, pl.ds(j, 1), :] = line_sum[:, taps + lags :]
        wide = weights.astype(jnp.float32)
        norm = jnp.sum(jnp.sum(wide * wide, axis=0, keepdims=True), axis=1, keepdims=True)
        CN[pl.ds(j, 1), :] = jnp.broadcast_to(norm, (1, CN.shape[1]))

    edge_send = remote(
        E.at[:, pl.ds(0, taps)], E.at[:, pl.ds(lags, taps)],
        tail_send.at[0], tail_recv.at[0], {"tm": me - 1},
    )

    def energies():
        own_traces.wait()
        for b in range(nblocks):
            part = X[core, b].astype(jnp.float32)
            E[pl.ds(b, 1), pl.ds(0, lags)] = jnp.sum(part * part, axis=0, keepdims=True)
        only(me > 0, edge_send.start)

        @pl.when(me + 1 == tm)
        def _():
            E[:, pl.ds(lags, taps)] = jnp.zeros((nblocks, taps), jnp.float32)

    def windows():
        only(me + 1 < tm, edge_send.wait_recv)
        window = E[...]
        reach = 1
        while reach < taps:
            window = window + pltpu.roll(window, window.shape[1] - reach, 1)
            reach *= 2
        for b in range(nblocks):
            WIN[b] = window[b : b + 1, :lags]
        for j in range(members):
            energy = WIN[listing[0, j]]
            for m in range(1, listed):
                energy = energy + WIN[listing[m, j]]
            EN[pl.ds(j, 1), :] = energy

    first, second = flows[:shared], flows[shared:]

    def stages(group, k):
        for flow in group:
            stage(flow, k)

    stages(first, 0)
    stages(second, 0)
    other_traces.start()
    energies()
    for k in range(1, line):
        stages(first, k)
        if k < line - 1:
            stages(second, k)
        if k == 1:
            windows()
    stages(first, line)
    other_traces.wait_recv()
    for i, flow in enumerate(first):
        correlate(flow[0])
        if i == 0:
            stages(second, line - 1)
    stages(second, line)
    for flow in second:
        correlate(flow[0])
    for j in theirs:
        passed(j)
        correlate(j)

    mate = remote(CC.at[1 - core], RC, tail_send.at[1], tail_recv.at[1], sibling)
    norms = remote(CN, RN, tail_send.at[2], tail_recv.at[2], sibling)
    before = remote(
        CP, RP.at[core], tail_send.at[3], tail_recv.at[3 + core], {"tm": 2 * chip - 1}
    )
    mate.start()
    norms.start()
    only(has_prev, before.start)
    mate.wait_recv()
    norms.wait_recv()

    mine_rows = pl.ds(pl.multiple_of(core * half, half), half)
    mate_rows = pl.ds(pl.multiple_of((1 - core) * half, half), half)

    takes = jnp.logical_and(has_next, core == 1)

    @pl.when(takes)
    def _():
        for c in range(2):
            remote(CP, RP.at[c], tail_send.at[3], tail_recv.at[3 + c], sibling).wait_recv()

    def finish(value, rows_, norm, tail):
        denominator = EN[rows_, :] * norm[:, :1] + epsilon
        factor = lax.rsqrt(denominator) * scale
        out[rows_, :] = value * factor

        @pl.when(takes)
        def _():
            last = pl.ds(lags - taps, taps)
            out[rows_, last] = (value[:, lags - taps :] + tail()) * factor[:, lags - taps :]

    finish(CC[core], mine_rows, CN[...], lambda: RP[core])
    finish(RC[...], mate_rows, RN[...], lambda: RP[1 - core])

    other_slab.wait_send()
    other_traces.wait_send()
    mate.wait_send()
    norms.wait_send()
    only(has_prev, before.wait_send)
    only(me > 0, edge_send.wait_send)
    for way, j, p, allowed in started:
        only(allowed, move(way, j, p).wait_send)


def fused(traces, templates, blocks):
    channels, lags = traces.shape
    local_taps, members, rows = templates.shape
    tm = lax.axis_size("tm")
    taps = local_taps * tm
    half = members // 2
    depth = rows // blocks.shape[1]
    nblocks = channels // depth
    chips = tm // 2
    vmem = pl.BlockSpec(memory_space=pltpu.VMEM)
    f32 = jnp.float32
    return pl.pallas_call(
        functools.partial(kernel, tm),
        out_shape=jax.ShapeDtypeStruct((members, lags), f32),
        in_specs=[
            pl.BlockSpec(memory_space=pltpu.SMEM),
            pl.BlockSpec(memory_space=pl.ANY),
            pl.BlockSpec(memory_space=pl.ANY),
        ],
        out_specs=vmem,
        scratch_shapes=[
            pltpu.VMEM(templates.shape, templates.dtype),
            pltpu.VMEM((2, nblocks, depth, lags), traces.dtype),
            pltpu.VMEM((half, taps, rows), templates.dtype),
            pltpu.VMEM((members, local_taps, rows), templates.dtype),
            pltpu.VMEM((half, taps), f32),
            pltpu.VMEM((2, half, lags), f32),
            pltpu.VMEM((half, 128), f32),
            pltpu.VMEM((half, lags), f32),
            pltpu.VMEM((half, 128), f32),
            pltpu.VMEM((2, half, taps), f32),
            pltpu.VMEM((nblocks, lags + taps), f32),
            pltpu.VMEM((nblocks, 1, lags), f32),
            pltpu.VMEM((members, lags), f32),
            pltpu.SemaphoreType.DMA,
            pltpu.SemaphoreType.DMA((3,)),
            pltpu.SemaphoreType.DMA((3,)),
            pltpu.SemaphoreType.DMA((4, half, chips)),
            pltpu.SemaphoreType.DMA((half, chips)),
            pltpu.SemaphoreType.DMA((4,)),
            pltpu.SemaphoreType.DMA((5,)),
        ],
        compiler_params=pltpu.CompilerParams(
            collective_id=0, has_side_effects=True, vmem_limit_bytes=60 * 2**20
        ),
    )(blocks.T, traces.reshape(nblocks, depth, lags), templates)


def per_device(traces, templates, blocks):
    channels, lags = traces.shape
    local_taps, members, rows = templates.shape
    tm = lax.axis_size("tm")
    taps = local_taps * tm
    fits = (
        lax.axis_size("span") == 2
        and tm % 4 == 0
        and local_taps % 16 == 0
        and members == 16
        and taps == 256
        and lags % 128 == 0
        and rows % (128 * blocks.shape[1]) == 0
    )
    return (fused if fits else plain)(traces, templates, blocks)


def solution(mesh):
    return jax.shard_map(
        per_device,
        mesh=mesh,
        in_specs=(P(None, ("span", "tm")), P("tm", None, None), P()),
        out_specs=P(None, ("span", "tm")),
        check_vma=False,
    )
```

```python
import functools
import math

import jax
import jax.numpy as jnp
from jax import lax
from jax.experimental import pallas as pl
from jax.experimental.pallas import tpu as pltpu
from jax.sharding import PartitionSpec as P

epsilon = 1e-06
MESH = pl.DeviceIdType.MESH


template_groups = 4


def from_behind(block, axis, distance):
    devices = range(lax.axis_size(axis))
    route = [(i - distance, i) for i in devices if i - distance in devices]
    return lax.ppermute(block, axis, route)


def tap_total(product, lag_count):
    members, tap_count, span_width = product.shape
    flattened = product.reshape(members, tap_count * span_width)
    flattened = jnp.pad(flattened, ((0, 0), (0, tap_count)))
    return flattened.reshape(members, tap_count, span_width + 1)[:, :, :lag_count].sum(axis=1)


def plain(traces, templates, blocks):
    channels, lag_count = traces.shape
    local_taps, members, row_count = templates.shape
    listed = blocks.shape[1]
    block_rows = row_count // listed
    nblocks = channels // block_rows
    tap_count = local_taps * lax.axis_size("tm")
    incoming = from_behind(traces[:, :tap_count], "tm", -1)
    source = jnp.concatenate([traces, incoming], axis=1)
    span_width = source.shape[1]
    squares = (
        jnp.square(source.astype(jnp.float32)).reshape(nblocks, block_rows, span_width).sum(axis=1)
    )
    running = jnp.concatenate(
        [jnp.zeros((nblocks, 1), jnp.float32), jnp.cumsum(squares, axis=1)], axis=1
    )
    window = running[:, tap_count : tap_count + lag_count] - running[:, :lag_count]
    selector = (blocks[:, :, None] == jnp.arange(nblocks, dtype=jnp.int32)[None, None, :]).astype(
        jnp.float32
    )
    counting = selector.sum(axis=1)
    scale_factor = math.sqrt(tap_count * row_count)
    group_size = members // template_groups
    gathered = lax.all_gather(templates, "tm", axis=0, tiled=True)
    pieces = []
    norm_pieces = []
    for group_index in range(template_groups):
        offset = group_index * group_size
        weights = gathered[:, offset : offset + group_size]
        chosen = source.reshape(nblocks, block_rows, span_width)[
            blocks[offset : offset + group_size]
        ]
        chosen = chosen.reshape(group_size, row_count, span_width)
        product = jnp.einsum("kqr,qrl->qkl", weights, chosen, preferred_element_type=jnp.float32)
        pieces.append(tap_total(product, lag_count))
        norm_pieces.append(jnp.sum(jnp.square(weights.astype(jnp.float32)), axis=(0, 2)))
    correlation = jnp.concatenate(pieces, axis=0)
    norm_sums = jnp.concatenate(norm_pieces, axis=0)
    energy = jnp.dot(counting, window, precision=lax.Precision.HIGHEST)
    denominator = energy * norm_sums[:, None] + epsilon
    return correlation * lax.rsqrt(denominator) * scale_factor


def only(condition, action):
    if condition is None:
        action()
        return

    @pl.when(condition)
    def _():
        action()


UP, DOWN, ACROSS, PLANE = range(4)


def kernel(
    tm,
    listing, traces, templates, out,
    T, X, W, S, CP, CC, CN, RC, RN, RP, E, WIN, EN, PA, PB,
    t_sem, x_sem, slab_sem, send_sem, recv_sem, tail_send, tail_recv,
):
    nblocks, depth, lags = traces.shape
    local_taps, members, rows = templates.shape
    listed = listing.shape[0]
    taps = local_taps * tm
    half = members // 2
    pair_taps = 2 * local_taps
    line = tm // 4
    chips = tm // 2
    shared = (3 * half // 4) // 2
    scale = math.sqrt(taps * rows)

    me = lax.axis_index("tm")
    plane = lax.axis_index("span")
    core = lax.rem(me, 2)
    chip = me // 2
    x = lax.rem(chip, 2)
    z = chip // 2

    def device(z_, x_, c_):
        return {"tm": (z_ * 2 + x_) * 2 + c_}

    sibling = device(z, x, 1 - core)
    targets = {
        UP: device(z + 1, x, core),
        DOWN: device(z - 1, x, core),
        ACROSS: device(z, 1 - x, core),
        PLANE: {"span": 1 - plane},
    }
    has_up, has_down = z + 1 < line, z > 0
    has_next, has_prev = chip + 1 < chips, chip > 0

    own_templates = pltpu.make_async_copy(templates, T, t_sem)
    own_templates.start()

    barrier = pltpu.get_barrier_semaphore()

    def greet(target):
        pl.semaphore_signal(barrier, inc=1, device_id=target, device_id_type=MESH)

    greet(sibling)
    greet(targets[ACROSS])
    greet(targets[PLANE])
    only(has_up, lambda: greet(targets[UP]))
    only(has_down, lambda: greet(targets[DOWN]))

    @pl.when(jnp.logical_and(has_next, core == 1))
    def _():
        greet({"tm": 2 * chip + 2})
        greet({"tm": 2 * chip + 3})

    own_traces = pltpu.make_async_copy(traces, X.at[core], x_sem.at[0])
    own_traces.start()
    own_templates.wait()
    S[...] = jnp.swapaxes(T[...], 0, 1)
    slab_rows = pl.ds(pl.multiple_of(me * local_taps, local_taps), local_taps)
    own_slab = pltpu.make_async_copy(
        S.at[pl.ds(core * half, half)], W.at[:, slab_rows, :], slab_sem.at[0]
    )
    own_slab.start()

    greetings = 3 + has_up.astype(jnp.int32) + has_down.astype(jnp.int32) + has_prev.astype(jnp.int32)
    pl.semaphore_wait(barrier, greetings)

    def remote(src, dst, send, recv, target):
        return pltpu.make_async_remote_copy(
            src_ref=src, dst_ref=dst, send_sem=send, recv_sem=recv,
            device_id=target, device_id_type=MESH,
        )

    other_slab = remote(
        S.at[pl.ds((1 - core) * half, half)], W.at[:, slab_rows, :],
        slab_sem.at[1], slab_sem.at[2], sibling,
    )
    other_slab.start()
    other_traces = remote(traces, X.at[core], x_sem.at[1], x_sem.at[2], sibling)

    started = []

    def move(way, j, p):
        part = W.at[j, pl.ds(pl.multiple_of(p * pair_taps, pair_taps), pair_taps), :]
        return remote(part, part, send_sem.at[way, j, p], recv_sem.at[j, p], targets[way])

    def send(way, j, p, allowed):
        started.append((way, j, p, allowed))
        only(allowed, lambda: move(way, j, p).start())

    def arrived(j, p, allowed):
        only(allowed, lambda: move(ACROSS, j, p).wait_recv())

    own_slab.wait()
    other_slab.wait_recv()

    mine = [plane * shared + i for i in range(shared)]
    theirs = [(1 - plane) * shared + i for i in range(shared)]
    both = list(range(2 * shared, half))
    flows = [(j, True) for j in mine] + [(j, False) for j in both]
    always = None

    def stage(flow, k):
        j, passed_on = flow
        here = lambda d: (z + d) * 2 + x
        there = lambda d: (z + d) * 2 + 1 - x
        if k == 0:
            send(UP, j, here(0), has_up)
            send(DOWN, j, here(0), has_down)
            send(ACROSS, j, here(0), always)
            return
        if k < line:
            below, above = z >= k, z + k < line
            arrived(j, here(-k), below)
            send(UP, j, here(-k), jnp.logical_and(below, has_up))
            send(ACROSS, j, here(-k), below)
            if passed_on:
                send(PLANE, j, here(-k), below)
            arrived(j, here(k), above)
            send(DOWN, j, here(k), jnp.logical_and(above, has_down))
            send(ACROSS, j, here(k), above)
            if passed_on:
                send(PLANE, j, here(k), above)
        d = k - 1
        if d == 0:
            arrived(j, there(0), always)
            if passed_on:
                send(PLANE, j, there(0), always)
        else:
            below, above = z >= d, z + d < line
            arrived(j, there(-d), below)
            if passed_on:
                send(PLANE, j, there(-d), below)
            arrived(j, there(d), above)
            if passed_on:
                send(PLANE, j, there(d), above)

    def passed(j):
        for d in range(1, chips):
            arrived(j, lax.rem(chip + d, chips), always)

    tile = 256
    half_taps = taps // 2
    pieces = lags // tile
    bands = half_taps // 8 // pieces
    unit = {"count": 0, "open": None, "partial": []}

    def multiply(j, h, n, slot):
        names = [listing[m, core * half + j] for m in range(listed)]
        chosen = jnp.concatenate([X[h, b, :, pl.ds(n * tile, tile)] for b in names], axis=0)
        slot[:, pl.ds(n * tile, tile)] = jnp.dot(W[j], chosen, preferred_element_type=jnp.float32)

    def shear(n, slot, total):
        for band in range(n * bands, (n + 1) * bands):
            row = 8 * band
            near = slot[pl.ds(row, 8), :]
            far = slot[pl.ds(row + half_taps, 8), :]
            gap = jnp.zeros((8, half_taps), jnp.float32)
            joined = jnp.concatenate([far, gap], axis=1) + jnp.concatenate([gap, near], axis=1)
            joined = jnp.concatenate([gap, joined], axis=1)
            if row:
                joined = pltpu.roll(joined, joined.shape[1] - row, 1)
            total = joined if total is None else total + joined
        return total

    def store(j):
        gap = jnp.zeros((8, lags), jnp.float32)
        low, high = unit["partial"]
        unit["partial"] = []
        sheared = jnp.concatenate([low, gap], axis=1) + jnp.concatenate([gap, high], axis=1)
        row_index = lax.broadcasted_iota(jnp.int32, sheared.shape, 0)
        for bit in (1, 2, 4):
            moved = pltpu.roll(sheared, sheared.shape[1] - bit, 1)
            sheared = jnp.where(lax.rem(row_index // bit, 2) == 1, moved, sheared)
        line_sum = jnp.sum(sheared, axis=0, keepdims=True)
        CP[pl.ds(j, 1), :] = line_sum[:, :taps]
        CC[0, pl.ds(j, 1), :] = line_sum[:, taps : taps + lags]
        CC[1, pl.ds(j, 1), :] = line_sum[:, taps + lags :]

    def advance(new):
        old = unit["open"]
        slots = (PA, PB) if unit["count"] % 2 == 0 else (PB, PA)
        total = None
        for n in range(pieces):
            if new is not None:
                multiply(*new, n, slots[0])
            if old is not None:
                total = shear(n, slots[1], total)
        if old is not None:
            unit["partial"].append(total)
            if old[1] == 1:
                store(old[0])
        unit["open"] = new
        unit["count"] += 1

    def correlate(j):
        advance((j, 0))
        wide = W[j].astype(jnp.float32)
        norm = jnp.sum(jnp.sum(wide * wide, axis=0, keepdims=True), axis=1, keepdims=True)
        CN[pl.ds(j, 1), :] = jnp.broadcast_to(norm, (1, CN.shape[1]))
        advance((j, 1))

    edge_send = remote(
        E.at[:, pl.ds(0, taps)], E.at[:, pl.ds(lags, taps)],
        tail_send.at[0], tail_recv.at[0], {"tm": me - 1},
    )

    def energies():
        own_traces.wait()
        for b in range(nblocks):
            part = X[core, b].astype(jnp.float32)
            E[pl.ds(b, 1), pl.ds(0, lags)] = jnp.sum(part * part, axis=0, keepdims=True)
        only(me > 0, edge_send.start)

        @pl.when(me + 1 == tm)
        def _():
            E[:, pl.ds(lags, taps)] = jnp.zeros((nblocks, taps), jnp.float32)

    def windows():
        only(me + 1 < tm, edge_send.wait_recv)
        window = E[...]
        reach = 1
        while reach < taps:
            window = window + pltpu.roll(window, window.shape[1] - reach, 1)
            reach *= 2
        for b in range(nblocks):
            WIN[b] = window[b : b + 1, :lags]
        for j in range(members):
            energy = WIN[listing[0, j]]
            for m in range(1, listed):
                energy = energy + WIN[listing[m, j]]
            EN[pl.ds(j, 1), :] = energy

    first, second = flows[:shared], flows[shared:]

    def stages(group, k):
        for flow in group:
            stage(flow, k)

    stages(first, 0)
    stages(second, 0)
    other_traces.start()
    energies()
    for k in range(1, line):
        stages(first, k)
        if k < line - 1:
            stages(second, k)
        if k == 1:
            windows()
    stages(first, line)
    other_traces.wait_recv()
    for i, flow in enumerate(first):
        correlate(flow[0])
        if i == 0:
            stages(second, line - 1)
    stages(second, line)
    for flow in second:
        correlate(flow[0])
    for j in theirs:
        passed(j)
        correlate(j)
    advance(None)

    mate = remote(CC.at[1 - core], RC, tail_send.at[1], tail_recv.at[1], sibling)
    norms = remote(CN, RN, tail_send.at[2], tail_recv.at[2], sibling)
    before = remote(
        CP, RP.at[core], tail_send.at[3], tail_recv.at[3 + core], {"tm": 2 * chip - 1}
    )
    mate.start()
    norms.start()
    only(has_prev, before.start)
    mate.wait_recv()
    norms.wait_recv()

    mine_rows = pl.ds(pl.multiple_of(core * half, half), half)
    mate_rows = pl.ds(pl.multiple_of((1 - core) * half, half), half)

    takes = jnp.logical_and(has_next, core == 1)

    @pl.when(takes)
    def _():
        for c in range(2):
            remote(CP, RP.at[c], tail_send.at[3], tail_recv.at[3 + c], sibling).wait_recv()

    def finish(value, rows_, norm, tail):
        denominator = EN[rows_, :] * norm[:, :1] + epsilon
        factor = lax.rsqrt(denominator) * scale
        out[rows_, :] = value * factor

        @pl.when(takes)
        def _():
            last = pl.ds(lags - taps, taps)
            out[rows_, last] = (value[:, lags - taps :] + tail()) * factor[:, lags - taps :]

    finish(CC[core], mine_rows, CN[...], lambda: RP[core])
    finish(RC[...], mate_rows, RN[...], lambda: RP[1 - core])

    other_slab.wait_send()
    other_traces.wait_send()
    mate.wait_send()
    norms.wait_send()
    only(has_prev, before.wait_send)
    only(me > 0, edge_send.wait_send)
    for way, j, p, allowed in started:
        only(allowed, move(way, j, p).wait_send)


def fused(traces, templates, blocks):
    channels, lags = traces.shape
    local_taps, members, rows = templates.shape
    tm = lax.axis_size("tm")
    taps = local_taps * tm
    half = members // 2
    depth = rows // blocks.shape[1]
    nblocks = channels // depth
    chips = tm // 2
    vmem = pl.BlockSpec(memory_space=pltpu.VMEM)
    f32 = jnp.float32
    return pl.pallas_call(
        functools.partial(kernel, tm),
        out_shape=jax.ShapeDtypeStruct((members, lags), f32),
        in_specs=[
            pl.BlockSpec(memory_space=pltpu.SMEM),
            pl.BlockSpec(memory_space=pl.ANY),
            pl.BlockSpec(memory_space=pl.ANY),
        ],
        out_specs=vmem,
        scratch_shapes=[
            pltpu.VMEM(templates.shape, templates.dtype),
            pltpu.VMEM((2, nblocks, depth, lags), traces.dtype),
            pltpu.VMEM((half, taps, rows), templates.dtype),
            pltpu.VMEM((members, local_taps, rows), templates.dtype),
            pltpu.VMEM((half, taps), f32),
            pltpu.VMEM((2, half, lags), f32),
            pltpu.VMEM((half, 128), f32),
            pltpu.VMEM((half, lags), f32),
            pltpu.VMEM((half, 128), f32),
            pltpu.VMEM((2, half, taps), f32),
            pltpu.VMEM((nblocks, lags + taps), f32),
            pltpu.VMEM((nblocks, 1, lags), f32),
            pltpu.VMEM((members, lags), f32),
            pltpu.VMEM((taps, lags), f32),
            pltpu.VMEM((taps, lags), f32),
            pltpu.SemaphoreType.DMA,
            pltpu.SemaphoreType.DMA((3,)),
            pltpu.SemaphoreType.DMA((3,)),
            pltpu.SemaphoreType.DMA((4, half, chips)),
            pltpu.SemaphoreType.DMA((half, chips)),
            pltpu.SemaphoreType.DMA((4,)),
            pltpu.SemaphoreType.DMA((5,)),
        ],
        compiler_params=pltpu.CompilerParams(
            collective_id=0, has_side_effects=True, vmem_limit_bytes=60 * 2**20
        ),
    )(blocks.T, traces.reshape(nblocks, depth, lags), templates)


def per_device(traces, templates, blocks):
    channels, lags = traces.shape
    local_taps, members, rows = templates.shape
    tm = lax.axis_size("tm")
    taps = local_taps * tm
    fits = (
        lax.axis_size("span") == 2
        and tm % 4 == 0
        and local_taps % 16 == 0
        and members == 16
        and taps == 256
        and lags % 256 == 0
        and (taps // 16) % (lags // 256) == 0
        and rows % (128 * blocks.shape[1]) == 0
    )
    return (fused if fits else plain)(traces, templates, blocks)


def solution(mesh):
    return jax.shard_map(
        per_device,
        mesh=mesh,
        in_specs=(P(None, ("span", "tm")), P("tm", None, None), P()),
        out_specs=P(None, ("span", "tm")),
        check_vma=False,
    )
```

```python
import functools
import math

import jax
import jax.numpy as jnp
from jax import lax
from jax.experimental import pallas as pl
from jax.experimental.pallas import tpu as pltpu
from jax.sharding import PartitionSpec as P

epsilon = 1e-06
MESH = pl.DeviceIdType.MESH


template_groups = 4


def from_behind(block, axis, distance):
    devices = range(lax.axis_size(axis))
    route = [(i - distance, i) for i in devices if i - distance in devices]
    return lax.ppermute(block, axis, route)


def tap_total(product, lag_count):
    members, tap_count, span_width = product.shape
    flattened = product.reshape(members, tap_count * span_width)
    flattened = jnp.pad(flattened, ((0, 0), (0, tap_count)))
    return flattened.reshape(members, tap_count, span_width + 1)[:, :, :lag_count].sum(axis=1)


def plain(traces, templates, blocks):
    channels, lag_count = traces.shape
    local_taps, members, row_count = templates.shape
    listed = blocks.shape[1]
    block_rows = row_count // listed
    nblocks = channels // block_rows
    tap_count = local_taps * lax.axis_size("tm")
    incoming = from_behind(traces[:, :tap_count], "tm", -1)
    source = jnp.concatenate([traces, incoming], axis=1)
    span_width = source.shape[1]
    squares = (
        jnp.square(source.astype(jnp.float32)).reshape(nblocks, block_rows, span_width).sum(axis=1)
    )
    running = jnp.concatenate(
        [jnp.zeros((nblocks, 1), jnp.float32), jnp.cumsum(squares, axis=1)], axis=1
    )
    window = running[:, tap_count : tap_count + lag_count] - running[:, :lag_count]
    selector = (blocks[:, :, None] == jnp.arange(nblocks, dtype=jnp.int32)[None, None, :]).astype(
        jnp.float32
    )
    counting = selector.sum(axis=1)
    scale_factor = math.sqrt(tap_count * row_count)
    group_size = members // template_groups
    gathered = lax.all_gather(templates, "tm", axis=0, tiled=True)
    pieces = []
    norm_pieces = []
    for group_index in range(template_groups):
        offset = group_index * group_size
        weights = gathered[:, offset : offset + group_size]
        chosen = source.reshape(nblocks, block_rows, span_width)[
            blocks[offset : offset + group_size]
        ]
        chosen = chosen.reshape(group_size, row_count, span_width)
        product = jnp.einsum("kqr,qrl->qkl", weights, chosen, preferred_element_type=jnp.float32)
        pieces.append(tap_total(product, lag_count))
        norm_pieces.append(jnp.sum(jnp.square(weights.astype(jnp.float32)), axis=(0, 2)))
    correlation = jnp.concatenate(pieces, axis=0)
    norm_sums = jnp.concatenate(norm_pieces, axis=0)
    energy = jnp.dot(counting, window, precision=lax.Precision.HIGHEST)
    denominator = energy * norm_sums[:, None] + epsilon
    return correlation * lax.rsqrt(denominator) * scale_factor


def only(condition, action):
    if condition is None:
        action()
        return

    @pl.when(condition)
    def _():
        action()


UP, DOWN, ACROSS, PLANE = range(4)


def kernel(
    tm,
    listing, traces, templates, out,
    T, X, W, S, CP, CC, CN, RC, RN, RP, E, WIN, EN, PA, PB,
    t_sem, x_sem, slab_sem, send_sem, recv_sem, tail_send, tail_recv,
):
    nblocks, depth, lags = traces.shape
    local_taps, members, rows = templates.shape
    listed = listing.shape[0]
    taps = local_taps * tm
    half = members // 2
    pair_taps = 2 * local_taps
    line = tm // 4
    chips = tm // 2
    shared = (3 * half // 4) // 2
    scale = math.sqrt(taps * rows)

    me = lax.axis_index("tm")
    plane = lax.axis_index("span")
    core = lax.rem(me, 2)
    chip = me // 2
    x = lax.rem(chip, 2)
    z = chip // 2

    def device(z_, x_, c_):
        return {"tm": (z_ * 2 + x_) * 2 + c_}

    sibling = device(z, x, 1 - core)
    targets = {
        UP: device(z + 1, x, core),
        DOWN: device(z - 1, x, core),
        ACROSS: device(z, 1 - x, core),
        PLANE: {"span": 1 - plane},
    }
    has_up, has_down = z + 1 < line, z > 0
    has_next, has_prev = chip + 1 < chips, chip > 0

    own_templates = pltpu.make_async_copy(templates, T, t_sem)
    own_templates.start()

    barrier = pltpu.get_barrier_semaphore()

    def greet(target):
        pl.semaphore_signal(barrier, inc=1, device_id=target, device_id_type=MESH)

    greet(sibling)
    greet(targets[ACROSS])
    greet(targets[PLANE])
    only(has_up, lambda: greet(targets[UP]))
    only(has_down, lambda: greet(targets[DOWN]))

    @pl.when(jnp.logical_and(has_next, core == 1))
    def _():
        greet({"tm": 2 * chip + 2})
        greet({"tm": 2 * chip + 3})

    own_traces = pltpu.make_async_copy(traces, X.at[core], x_sem.at[0])
    own_traces.start()
    own_templates.wait()
    S[...] = jnp.swapaxes(T[...], 0, 1)
    slab_rows = pl.ds(pl.multiple_of(me * local_taps, local_taps), local_taps)
    own_slab = pltpu.make_async_copy(
        S.at[pl.ds(core * half, half)], W.at[:, slab_rows, :], slab_sem.at[0]
    )
    own_slab.start()

    greetings = 3 + has_up.astype(jnp.int32) + has_down.astype(jnp.int32) + has_prev.astype(jnp.int32)
    pl.semaphore_wait(barrier, greetings)

    def remote(src, dst, send, recv, target):
        return pltpu.make_async_remote_copy(
            src_ref=src, dst_ref=dst, send_sem=send, recv_sem=recv,
            device_id=target, device_id_type=MESH,
        )

    other_slab = remote(
        S.at[pl.ds((1 - core) * half, half)], W.at[:, slab_rows, :],
        slab_sem.at[1], slab_sem.at[2], sibling,
    )
    other_slab.start()
    other_traces = remote(traces, X.at[core], x_sem.at[1], x_sem.at[2], sibling)

    started = []

    first = (plane * shared, shared, plane, True)
    theirs = ((1 - plane) * shared, shared, 1 - plane, False)
    second = (2 * shared, half - 2 * shared, 2, False)

    def move(way, group, p):
        start, count, mark, _ = group
        part = W.at[
            pl.ds(start, count), pl.ds(pl.multiple_of(p * pair_taps, pair_taps), pair_taps), :
        ]
        return remote(part, part, send_sem.at[way, mark, p], recv_sem.at[mark, p], targets[way])

    def send(way, group, p, allowed):
        started.append((way, group, p, allowed))
        only(allowed, lambda: move(way, group, p).start())

    def arrived(group, p, allowed):
        only(allowed, lambda: move(ACROSS, group, p).wait_recv())

    own_slab.wait()
    other_slab.wait_recv()

    always = None

    def stage(j, k):
        passed_on = j[3]
        here = lambda d: (z + d) * 2 + x
        there = lambda d: (z + d) * 2 + 1 - x
        if k == 0:
            send(UP, j, here(0), has_up)
            send(DOWN, j, here(0), has_down)
            send(ACROSS, j, here(0), always)
            return
        if k < line:
            below, above = z >= k, z + k < line
            arrived(j, here(-k), below)
            send(UP, j, here(-k), jnp.logical_and(below, has_up))
            send(ACROSS, j, here(-k), below)
            if passed_on:
                send(PLANE, j, here(-k), below)
            arrived(j, here(k), above)
            send(DOWN, j, here(k), jnp.logical_and(above, has_down))
            send(ACROSS, j, here(k), above)
            if passed_on:
                send(PLANE, j, here(k), above)
        d = k - 1
        if d == 0:
            arrived(j, there(0), always)
            if passed_on:
                send(PLANE, j, there(0), always)
        else:
            below, above = z >= d, z + d < line
            arrived(j, there(-d), below)
            if passed_on:
                send(PLANE, j, there(-d), below)
            arrived(j, there(d), above)
            if passed_on:
                send(PLANE, j, there(d), above)

    def passed(j):
        for d in range(1, chips):
            arrived(j, lax.rem(chip + d, chips), always)

    tile = 256
    half_taps = taps // 2
    pieces = lags // tile
    bands = half_taps // 8 // pieces
    unit = {"count": 0, "open": None, "partial": []}

    def multiply(j, h, n, slot):
        names = [listing[m, core * half + j] for m in range(listed)]
        chosen = jnp.concatenate([X[h, b, :, pl.ds(n * tile, tile)] for b in names], axis=0)
        slot[:, pl.ds(n * tile, tile)] = jnp.dot(W[j], chosen, preferred_element_type=jnp.float32)

    def shear(n, slot, total):
        for band in range(n * bands, (n + 1) * bands):
            row = 8 * band
            near = slot[pl.ds(row, 8), :]
            far = slot[pl.ds(row + half_taps, 8), :]
            gap = jnp.zeros((8, half_taps), jnp.float32)
            joined = jnp.concatenate([far, gap], axis=1) + jnp.concatenate([gap, near], axis=1)
            joined = jnp.concatenate([gap, joined], axis=1)
            if row:
                joined = pltpu.roll(joined, joined.shape[1] - row, 1)
            total = joined if total is None else total + joined
        return total

    def store(j):
        gap = jnp.zeros((8, lags), jnp.float32)
        low, high = unit["partial"]
        unit["partial"] = []
        sheared = jnp.concatenate([low, gap], axis=1) + jnp.concatenate([gap, high], axis=1)
        row_index = lax.broadcasted_iota(jnp.int32, sheared.shape, 0)
        for bit in (1, 2, 4):
            moved = pltpu.roll(sheared, sheared.shape[1] - bit, 1)
            sheared = jnp.where(lax.rem(row_index // bit, 2) == 1, moved, sheared)
        line_sum = jnp.sum(sheared, axis=0, keepdims=True)
        CP[pl.ds(j, 1), :] = line_sum[:, :taps]
        CC[0, pl.ds(j, 1), :] = line_sum[:, taps : taps + lags]
        CC[1, pl.ds(j, 1), :] = line_sum[:, taps + lags :]

    def advance(new):
        old = unit["open"]
        slots = (PA, PB) if unit["count"] % 2 == 0 else (PB, PA)
        total = None
        for n in range(pieces):
            if new is not None:
                multiply(*new, n, slots[0])
            if old is not None:
                total = shear(n, slots[1], total)
        if old is not None:
            unit["partial"].append(total)
            if old[1] == 1:
                store(old[0])
        unit["open"] = new
        unit["count"] += 1

    def correlate(j):
        advance((j, 0))
        wide = W[j].astype(jnp.float32)
        norm = jnp.sum(jnp.sum(wide * wide, axis=0, keepdims=True), axis=1, keepdims=True)
        CN[pl.ds(j, 1), :] = jnp.broadcast_to(norm, (1, CN.shape[1]))
        advance((j, 1))

    edge_send = remote(
        E.at[:, pl.ds(0, taps)], E.at[:, pl.ds(lags, taps)],
        tail_send.at[0], tail_recv.at[0], {"tm": me - 1},
    )

    def energies():
        own_traces.wait()
        for b in range(nblocks):
            part = X[core, b].astype(jnp.float32)
            E[pl.ds(b, 1), pl.ds(0, lags)] = jnp.sum(part * part, axis=0, keepdims=True)
        only(me > 0, edge_send.start)

        @pl.when(me + 1 == tm)
        def _():
            E[:, pl.ds(lags, taps)] = jnp.zeros((nblocks, taps), jnp.float32)

    def windows():
        only(me + 1 < tm, edge_send.wait_recv)
        window = E[...]
        reach = 1
        while reach < taps:
            window = window + pltpu.roll(window, window.shape[1] - reach, 1)
            reach *= 2
        for b in range(nblocks):
            WIN[b] = window[b : b + 1, :lags]
        for j in range(members):
            energy = WIN[listing[0, j]]
            for m in range(1, listed):
                energy = energy + WIN[listing[m, j]]
            EN[pl.ds(j, 1), :] = energy

    stage(first, 0)
    stage(second, 0)
    other_traces.start()
    energies()
    for k in range(1, line):
        stage(first, k)
        if k < line - 1:
            stage(second, k)
        if k == 1:
            windows()
    stage(first, line)
    other_traces.wait_recv()
    for i in range(shared):
        correlate(first[0] + i)
        if i == 0:
            stage(second, line - 1)
    stage(second, line)
    for i in range(second[1]):
        correlate(second[0] + i)
    passed(theirs)
    for i in range(shared):
        correlate(theirs[0] + i)
    advance(None)

    mate = remote(CC.at[1 - core], RC, tail_send.at[1], tail_recv.at[1], sibling)
    norms = remote(CN, RN, tail_send.at[2], tail_recv.at[2], sibling)
    before = remote(
        CP, RP.at[core], tail_send.at[3], tail_recv.at[3 + core], {"tm": 2 * chip - 1}
    )
    mate.start()
    norms.start()
    only(has_prev, before.start)
    mate.wait_recv()
    norms.wait_recv()

    mine_rows = pl.ds(pl.multiple_of(core * half, half), half)
    mate_rows = pl.ds(pl.multiple_of((1 - core) * half, half), half)

    takes = jnp.logical_and(has_next, core == 1)

    @pl.when(takes)
    def _():
        for c in range(2):
            remote(CP, RP.at[c], tail_send.at[3], tail_recv.at[3 + c], sibling).wait_recv()

    def finish(value, rows_, norm, tail):
        denominator = EN[rows_, :] * norm[:, :1] + epsilon
        factor = lax.rsqrt(denominator) * scale
        out[rows_, :] = value * factor

        @pl.when(takes)
        def _():
            last = pl.ds(lags - taps, taps)
            out[rows_, last] = (value[:, lags - taps :] + tail()) * factor[:, lags - taps :]

    finish(CC[core], mine_rows, CN[...], lambda: RP[core])
    finish(RC[...], mate_rows, RN[...], lambda: RP[1 - core])

    other_slab.wait_send()
    other_traces.wait_send()
    mate.wait_send()
    norms.wait_send()
    only(has_prev, before.wait_send)
    only(me > 0, edge_send.wait_send)
    for way, j, p, allowed in started:
        only(allowed, move(way, j, p).wait_send)


def fused(traces, templates, blocks):
    channels, lags = traces.shape
    local_taps, members, rows = templates.shape
    tm = lax.axis_size("tm")
    taps = local_taps * tm
    half = members // 2
    depth = rows // blocks.shape[1]
    nblocks = channels // depth
    chips = tm // 2
    vmem = pl.BlockSpec(memory_space=pltpu.VMEM)
    f32 = jnp.float32
    return pl.pallas_call(
        functools.partial(kernel, tm),
        out_shape=jax.ShapeDtypeStruct((members, lags), f32),
        in_specs=[
            pl.BlockSpec(memory_space=pltpu.SMEM),
            pl.BlockSpec(memory_space=pl.ANY),
            pl.BlockSpec(memory_space=pl.ANY),
        ],
        out_specs=vmem,
        scratch_shapes=[
            pltpu.VMEM(templates.shape, templates.dtype),
            pltpu.VMEM((2, nblocks, depth, lags), traces.dtype),
            pltpu.VMEM((half, taps, rows), templates.dtype),
            pltpu.VMEM((members, local_taps, rows), templates.dtype),
            pltpu.VMEM((half, taps), f32),
            pltpu.VMEM((2, half, lags), f32),
            pltpu.VMEM((half, 128), f32),
            pltpu.VMEM((half, lags), f32),
            pltpu.VMEM((half, 128), f32),
            pltpu.VMEM((2, half, taps), f32),
            pltpu.VMEM((nblocks, lags + taps), f32),
            pltpu.VMEM((nblocks, 1, lags), f32),
            pltpu.VMEM((members, lags), f32),
            pltpu.VMEM((taps, lags), f32),
            pltpu.VMEM((taps, lags), f32),
            pltpu.SemaphoreType.DMA,
            pltpu.SemaphoreType.DMA((3,)),
            pltpu.SemaphoreType.DMA((3,)),
            pltpu.SemaphoreType.DMA((4, 3, chips)),
            pltpu.SemaphoreType.DMA((3, chips)),
            pltpu.SemaphoreType.DMA((4,)),
            pltpu.SemaphoreType.DMA((5,)),
        ],
        compiler_params=pltpu.CompilerParams(
            collective_id=0, has_side_effects=True, vmem_limit_bytes=60 * 2**20
        ),
    )(blocks.T, traces.reshape(nblocks, depth, lags), templates)


def per_device(traces, templates, blocks):
    channels, lags = traces.shape
    local_taps, members, rows = templates.shape
    tm = lax.axis_size("tm")
    taps = local_taps * tm
    fits = (
        lax.axis_size("span") == 2
        and tm % 4 == 0
        and local_taps % 16 == 0
        and members == 16
        and taps == 256
        and lags % 256 == 0
        and (taps // 16) % (lags // 256) == 0
        and rows % (128 * blocks.shape[1]) == 0
    )
    return (fused if fits else plain)(traces, templates, blocks)


def solution(mesh):
    return jax.shard_map(
        per_device,
        mesh=mesh,
        in_specs=(P(None, ("span", "tm")), P("tm", None, None), P()),
        out_specs=P(None, ("span", "tm")),
        check_vma=False,
    )
```

```python
import functools
import math

import jax
import jax.numpy as jnp
from jax import lax
from jax.experimental import pallas as pl
from jax.experimental.pallas import tpu as pltpu
from jax.sharding import PartitionSpec as P

epsilon = 1e-06
MESH = pl.DeviceIdType.MESH


template_groups = 4


def from_behind(block, axis, distance):
    devices = range(lax.axis_size(axis))
    route = [(i - distance, i) for i in devices if i - distance in devices]
    return lax.ppermute(block, axis, route)


def tap_total(product, lag_count):
    members, tap_count, span_width = product.shape
    flattened = product.reshape(members, tap_count * span_width)
    flattened = jnp.pad(flattened, ((0, 0), (0, tap_count)))
    return flattened.reshape(members, tap_count, span_width + 1)[:, :, :lag_count].sum(axis=1)


def plain(traces, templates, blocks):
    channels, lag_count = traces.shape
    local_taps, members, row_count = templates.shape
    listed = blocks.shape[1]
    block_rows = row_count // listed
    nblocks = channels // block_rows
    tap_count = local_taps * lax.axis_size("tm")
    incoming = from_behind(traces[:, :tap_count], "tm", -1)
    source = jnp.concatenate([traces, incoming], axis=1)
    span_width = source.shape[1]
    squares = (
        jnp.square(source.astype(jnp.float32)).reshape(nblocks, block_rows, span_width).sum(axis=1)
    )
    running = jnp.concatenate(
        [jnp.zeros((nblocks, 1), jnp.float32), jnp.cumsum(squares, axis=1)], axis=1
    )
    window = running[:, tap_count : tap_count + lag_count] - running[:, :lag_count]
    selector = (blocks[:, :, None] == jnp.arange(nblocks, dtype=jnp.int32)[None, None, :]).astype(
        jnp.float32
    )
    counting = selector.sum(axis=1)
    scale_factor = math.sqrt(tap_count * row_count)
    group_size = members // template_groups
    gathered = lax.all_gather(templates, "tm", axis=0, tiled=True)
    pieces = []
    norm_pieces = []
    for group_index in range(template_groups):
        offset = group_index * group_size
        weights = gathered[:, offset : offset + group_size]
        chosen = source.reshape(nblocks, block_rows, span_width)[
            blocks[offset : offset + group_size]
        ]
        chosen = chosen.reshape(group_size, row_count, span_width)
        product = jnp.einsum("kqr,qrl->qkl", weights, chosen, preferred_element_type=jnp.float32)
        pieces.append(tap_total(product, lag_count))
        norm_pieces.append(jnp.sum(jnp.square(weights.astype(jnp.float32)), axis=(0, 2)))
    correlation = jnp.concatenate(pieces, axis=0)
    norm_sums = jnp.concatenate(norm_pieces, axis=0)
    energy = jnp.dot(counting, window, precision=lax.Precision.HIGHEST)
    denominator = energy * norm_sums[:, None] + epsilon
    return correlation * lax.rsqrt(denominator) * scale_factor


def only(condition, action):
    if condition is None:
        action()
        return

    @pl.when(condition)
    def _():
        action()


UP, DOWN, ACROSS, PLANE = range(4)


def kernel(
    tm,
    listing, traces, templates, out,
    T, X, W, S, CP, CC, CN, RC, RN, RP, E, WIN, EN, PA, PB,
    t_sem, x_sem, slab_sem, send_sem, recv_sem, tail_send, tail_recv,
):
    nblocks, depth, lags = traces.shape
    local_taps, members, rows = templates.shape
    listed = listing.shape[0]
    taps = local_taps * tm
    half = members // 2
    pair_taps = 2 * local_taps
    line = tm // 4
    chips = tm // 2
    shared = (3 * half // 4) // 2
    scale = math.sqrt(taps * rows)

    me = lax.axis_index("tm")
    plane = lax.axis_index("span")
    core = lax.rem(me, 2)
    chip = me // 2
    x = lax.rem(chip, 2)
    z = chip // 2

    def device(z_, x_, c_):
        return {"tm": (z_ * 2 + x_) * 2 + c_}

    sibling = device(z, x, 1 - core)
    targets = {
        UP: device(z + 1, x, core),
        DOWN: device(z - 1, x, core),
        ACROSS: device(z, 1 - x, core),
        PLANE: {"span": 1 - plane},
    }
    has_up, has_down = z + 1 < line, z > 0
    has_next, has_prev = chip + 1 < chips, chip > 0

    own_templates = pltpu.make_async_copy(templates, T, t_sem)
    own_templates.start()

    barrier = pltpu.get_barrier_semaphore()

    def greet(target):
        pl.semaphore_signal(barrier, inc=1, device_id=target, device_id_type=MESH)

    greet(sibling)
    greet(targets[ACROSS])
    greet(targets[PLANE])
    only(has_up, lambda: greet(targets[UP]))
    only(has_down, lambda: greet(targets[DOWN]))

    @pl.when(jnp.logical_and(has_next, core == 1))
    def _():
        greet({"tm": 2 * chip + 2})
        greet({"tm": 2 * chip + 3})

    own_traces = pltpu.make_async_copy(traces, X.at[core], x_sem.at[0])
    own_traces.start()
    own_templates.wait()
    S[...] = jnp.swapaxes(T[...], 0, 1)
    slab_rows = pl.ds(pl.multiple_of(me * local_taps, local_taps), local_taps)
    own_slab = pltpu.make_async_copy(
        S.at[pl.ds(core * half, half)], W.at[:, slab_rows, :], slab_sem.at[0]
    )
    own_slab.start()

    greetings = 3 + has_up.astype(jnp.int32) + has_down.astype(jnp.int32) + has_prev.astype(jnp.int32)
    pl.semaphore_wait(barrier, greetings)

    def remote(src, dst, send, recv, target):
        return pltpu.make_async_remote_copy(
            src_ref=src, dst_ref=dst, send_sem=send, recv_sem=recv,
            device_id=target, device_id_type=MESH,
        )

    other_slab = remote(
        S.at[pl.ds((1 - core) * half, half)], W.at[:, slab_rows, :],
        slab_sem.at[1], slab_sem.at[2], sibling,
    )
    other_slab.start()
    other_traces = remote(traces, X.at[core], x_sem.at[1], x_sem.at[2], sibling)

    started = []

    def move(way, j, p):
        part = W.at[j, pl.ds(pl.multiple_of(p * pair_taps, pair_taps), pair_taps), :]
        return remote(part, part, send_sem.at[way, j, p], recv_sem.at[j, p], targets[way])

    def send(way, j, p, allowed):
        started.append((way, j, p, allowed))
        only(allowed, lambda: move(way, j, p).start())

    def arrived(j, p, allowed):
        only(allowed, lambda: move(ACROSS, j, p).wait_recv())

    own_slab.wait()
    other_slab.wait_recv()

    mine = [plane * shared + i for i in range(shared)]
    theirs = [(1 - plane) * shared + i for i in range(shared)]
    both = list(range(2 * shared, half))
    flows = [(j, True) for j in mine] + [(j, False) for j in both]
    always = None

    def stage(flow, k):
        j, passed_on = flow
        here = lambda d: (z + d) * 2 + x
        there = lambda d: (z + d) * 2 + 1 - x
        if k == 0:
            send(UP, j, here(0), has_up)
            send(DOWN, j, here(0), has_down)
            send(ACROSS, j, here(0), always)
            return
        if k < line:
            below, above = z >= k, z + k < line
            arrived(j, here(-k), below)
            send(UP, j, here(-k), jnp.logical_and(below, has_up))
            send(ACROSS, j, here(-k), below)
            if passed_on:
                send(PLANE, j, here(-k), below)
            arrived(j, here(k), above)
            send(DOWN, j, here(k), jnp.logical_and(above, has_down))
            send(ACROSS, j, here(k), above)
            if passed_on:
                send(PLANE, j, here(k), above)
        d = k - 1
        if d == 0:
            arrived(j, there(0), always)
            if passed_on:
                send(PLANE, j, there(0), always)
        else:
            below, above = z >= d, z + d < line
            arrived(j, there(-d), below)
            if passed_on:
                send(PLANE, j, there(-d), below)
            arrived(j, there(d), above)
            if passed_on:
                send(PLANE, j, there(d), above)

    def passed(j):
        for d in range(1, chips):
            arrived(j, lax.rem(chip + d, chips), always)

    tile = 256
    half_taps = taps // 2
    pieces = lags // tile
    bands = half_taps // 8 // pieces
    unit = {"count": 0, "open": None, "partial": []}

    def multiply(j, h, n, slot):
        names = [listing[m, core * half + j] for m in range(listed)]
        chosen = jnp.concatenate([X[h, b, :, pl.ds(n * tile, tile)] for b in names], axis=0)
        slot[:, pl.ds(n * tile, tile)] = jnp.dot(W[j], chosen, preferred_element_type=jnp.float32)

    def shear(n, slot, total):
        for band in range(n * bands, (n + 1) * bands):
            row = 8 * band
            near = slot[pl.ds(row, 8), :]
            far = slot[pl.ds(row + half_taps, 8), :]
            gap = jnp.zeros((8, half_taps), jnp.float32)
            joined = jnp.concatenate([far, gap], axis=1) + jnp.concatenate([gap, near], axis=1)
            joined = jnp.concatenate([gap, joined], axis=1)
            if row:
                joined = pltpu.roll(joined, joined.shape[1] - row, 1)
            total = joined if total is None else total + joined
        return total

    def store(j):
        gap = jnp.zeros((8, lags), jnp.float32)
        low, high = unit["partial"]
        unit["partial"] = []
        sheared = jnp.concatenate([low, gap], axis=1) + jnp.concatenate([gap, high], axis=1)
        row_index = lax.broadcasted_iota(jnp.int32, sheared.shape, 0)
        for bit in (1, 2, 4):
            moved = pltpu.roll(sheared, sheared.shape[1] - bit, 1)
            sheared = jnp.where(lax.rem(row_index // bit, 2) == 1, moved, sheared)
        line_sum = jnp.sum(sheared, axis=0, keepdims=True)
        CP[pl.ds(j, 1), :] = line_sum[:, :taps]
        CC[0, pl.ds(j, 1), :] = line_sum[:, taps : taps + lags]
        CC[1, pl.ds(j, 1), :] = line_sum[:, taps + lags :]

    def advance(new):
        old = unit["open"]
        slots = (PA, PB) if unit["count"] % 2 == 0 else (PB, PA)
        total = None
        for n in range(pieces):
            if new is not None:
                multiply(*new, n, slots[0])
            if old is not None:
                total = shear(n, slots[1], total)
        if old is not None:
            unit["partial"].append(total)
            if old[1] == 1:
                store(old[0])
        unit["open"] = new
        unit["count"] += 1

    def correlate(j, between=None):
        advance((j, 0))
        if between is not None:
            between()
        wide = W[j].astype(jnp.float32)
        norm = jnp.sum(jnp.sum(wide * wide, axis=0, keepdims=True), axis=1, keepdims=True)
        CN[pl.ds(j, 1), :] = jnp.broadcast_to(norm, (1, CN.shape[1]))
        advance((j, 1))

    edge_send = remote(
        E.at[:, pl.ds(0, taps)], E.at[:, pl.ds(lags, taps)],
        tail_send.at[0], tail_recv.at[0], {"tm": me - 1},
    )

    def energies():
        own_traces.wait()
        for b in range(nblocks):
            part = X[core, b].astype(jnp.float32)
            E[pl.ds(b, 1), pl.ds(0, lags)] = jnp.sum(part * part, axis=0, keepdims=True)
        only(me > 0, edge_send.start)

        @pl.when(me + 1 == tm)
        def _():
            E[:, pl.ds(lags, taps)] = jnp.zeros((nblocks, taps), jnp.float32)

    def windows():
        only(me + 1 < tm, edge_send.wait_recv)
        window = E[...]
        reach = 1
        while reach < taps:
            window = window + pltpu.roll(window, window.shape[1] - reach, 1)
            reach *= 2
        for b in range(nblocks):
            WIN[b] = window[b : b + 1, :lags]
        for j in range(members):
            energy = WIN[listing[0, j]]
            for m in range(1, listed):
                energy = energy + WIN[listing[m, j]]
            EN[pl.ds(j, 1), :] = energy

    first, second = flows[:shared], flows[shared:]

    def stages(group, k):
        for flow in group:
            stage(flow, k)

    stages(first, 0)
    other_traces.start()
    energies()
    stages(first, 1)
    stages(second, 0)
    for k in range(2, line):
        stages(first, k)
        stages(second, k - 1)
        if k == 2:
            windows()
    other_traces.wait_recv()
    stages(first[:1], line)

    def rest():
        stages(second, line - 1)
        stages(first[1:], line)

    for i, flow in enumerate(first):
        correlate(flow[0], rest if i == 0 else None)
    stages(second, line)
    for flow in second:
        correlate(flow[0])
    for j in theirs:
        passed(j)
        correlate(j)
    advance(None)

    mate = remote(CC.at[1 - core], RC, tail_send.at[1], tail_recv.at[1], sibling)
    norms = remote(CN, RN, tail_send.at[2], tail_recv.at[2], sibling)
    before = remote(
        CP, RP.at[core], tail_send.at[3], tail_recv.at[3 + core], {"tm": 2 * chip - 1}
    )
    mate.start()
    norms.start()
    only(has_prev, before.start)
    mate.wait_recv()
    norms.wait_recv()

    mine_rows = pl.ds(pl.multiple_of(core * half, half), half)
    mate_rows = pl.ds(pl.multiple_of((1 - core) * half, half), half)

    takes = jnp.logical_and(has_next, core == 1)

    @pl.when(takes)
    def _():
        for c in range(2):
            remote(CP, RP.at[c], tail_send.at[3], tail_recv.at[3 + c], sibling).wait_recv()

    def finish(value, rows_, norm, tail):
        denominator = EN[rows_, :] * norm[:, :1] + epsilon
        factor = lax.rsqrt(denominator) * scale
        out[rows_, :] = value * factor

        @pl.when(takes)
        def _():
            last = pl.ds(lags - taps, taps)
            out[rows_, last] = (value[:, lags - taps :] + tail()) * factor[:, lags - taps :]

    finish(CC[core], mine_rows, CN[...], lambda: RP[core])
    finish(RC[...], mate_rows, RN[...], lambda: RP[1 - core])

    other_slab.wait_send()
    other_traces.wait_send()
    mate.wait_send()
    norms.wait_send()
    only(has_prev, before.wait_send)
    only(me > 0, edge_send.wait_send)
    for way, j, p, allowed in started:
        only(allowed, move(way, j, p).wait_send)


def fused(traces, templates, blocks):
    channels, lags = traces.shape
    local_taps, members, rows = templates.shape
    tm = lax.axis_size("tm")
    taps = local_taps * tm
    half = members // 2
    depth = rows // blocks.shape[1]
    nblocks = channels // depth
    chips = tm // 2
    vmem = pl.BlockSpec(memory_space=pltpu.VMEM)
    f32 = jnp.float32
    return pl.pallas_call(
        functools.partial(kernel, tm),
        out_shape=jax.ShapeDtypeStruct((members, lags), f32),
        in_specs=[
            pl.BlockSpec(memory_space=pltpu.SMEM),
            pl.BlockSpec(memory_space=pl.ANY),
            pl.BlockSpec(memory_space=pl.ANY),
        ],
        out_specs=vmem,
        scratch_shapes=[
            pltpu.VMEM(templates.shape, templates.dtype),
            pltpu.VMEM((2, nblocks, depth, lags), traces.dtype),
            pltpu.VMEM((half, taps, rows), templates.dtype),
            pltpu.VMEM((members, local_taps, rows), templates.dtype),
            pltpu.VMEM((half, taps), f32),
            pltpu.VMEM((2, half, lags), f32),
            pltpu.VMEM((half, 128), f32),
            pltpu.VMEM((half, lags), f32),
            pltpu.VMEM((half, 128), f32),
            pltpu.VMEM((2, half, taps), f32),
            pltpu.VMEM((nblocks, lags + taps), f32),
            pltpu.VMEM((nblocks, 1, lags), f32),
            pltpu.VMEM((members, lags), f32),
            pltpu.VMEM((taps, lags), f32),
            pltpu.VMEM((taps, lags), f32),
            pltpu.SemaphoreType.DMA,
            pltpu.SemaphoreType.DMA((3,)),
            pltpu.SemaphoreType.DMA((3,)),
            pltpu.SemaphoreType.DMA((4, half, chips)),
            pltpu.SemaphoreType.DMA((half, chips)),
            pltpu.SemaphoreType.DMA((4,)),
            pltpu.SemaphoreType.DMA((5,)),
        ],
        compiler_params=pltpu.CompilerParams(
            collective_id=0, has_side_effects=True, vmem_limit_bytes=60 * 2**20
        ),
    )(blocks.T, traces.reshape(nblocks, depth, lags), templates)


def per_device(traces, templates, blocks):
    channels, lags = traces.shape
    local_taps, members, rows = templates.shape
    tm = lax.axis_size("tm")
    taps = local_taps * tm
    fits = (
        lax.axis_size("span") == 2
        and tm % 4 == 0
        and local_taps % 16 == 0
        and members == 16
        and taps == 256
        and lags % 256 == 0
        and (taps // 16) % (lags // 256) == 0
        and rows % (128 * blocks.shape[1]) == 0
    )
    return (fused if fits else plain)(traces, templates, blocks)


def solution(mesh):
    return jax.shard_map(
        per_device,
        mesh=mesh,
        in_specs=(P(None, ("span", "tm")), P("tm", None, None), P()),
        out_specs=P(None, ("span", "tm")),
        check_vma=False,
    )
```

```python
import functools
import math

import jax
import jax.numpy as jnp
from jax import lax
from jax.experimental import pallas as pl
from jax.experimental.pallas import tpu as pltpu
from jax.sharding import PartitionSpec as P

epsilon = 1e-06
MESH = pl.DeviceIdType.MESH


template_groups = 4


def from_behind(block, axis, distance):
    devices = range(lax.axis_size(axis))
    route = [(i - distance, i) for i in devices if i - distance in devices]
    return lax.ppermute(block, axis, route)


def tap_total(product, lag_count):
    members, tap_count, span_width = product.shape
    flattened = product.reshape(members, tap_count * span_width)
    flattened = jnp.pad(flattened, ((0, 0), (0, tap_count)))
    return flattened.reshape(members, tap_count, span_width + 1)[:, :, :lag_count].sum(axis=1)


def plain(traces, templates, blocks):
    channels, lag_count = traces.shape
    local_taps, members, row_count = templates.shape
    listed = blocks.shape[1]
    block_rows = row_count // listed
    nblocks = channels // block_rows
    tap_count = local_taps * lax.axis_size("tm")
    incoming = from_behind(traces[:, :tap_count], "tm", -1)
    source = jnp.concatenate([traces, incoming], axis=1)
    span_width = source.shape[1]
    squares = (
        jnp.square(source.astype(jnp.float32)).reshape(nblocks, block_rows, span_width).sum(axis=1)
    )
    running = jnp.concatenate(
        [jnp.zeros((nblocks, 1), jnp.float32), jnp.cumsum(squares, axis=1)], axis=1
    )
    window = running[:, tap_count : tap_count + lag_count] - running[:, :lag_count]
    selector = (blocks[:, :, None] == jnp.arange(nblocks, dtype=jnp.int32)[None, None, :]).astype(
        jnp.float32
    )
    counting = selector.sum(axis=1)
    scale_factor = math.sqrt(tap_count * row_count)
    group_size = members // template_groups
    gathered = lax.all_gather(templates, "tm", axis=0, tiled=True)
    pieces = []
    norm_pieces = []
    for group_index in range(template_groups):
        offset = group_index * group_size
        weights = gathered[:, offset : offset + group_size]
        chosen = source.reshape(nblocks, block_rows, span_width)[
            blocks[offset : offset + group_size]
        ]
        chosen = chosen.reshape(group_size, row_count, span_width)
        product = jnp.einsum("kqr,qrl->qkl", weights, chosen, preferred_element_type=jnp.float32)
        pieces.append(tap_total(product, lag_count))
        norm_pieces.append(jnp.sum(jnp.square(weights.astype(jnp.float32)), axis=(0, 2)))
    correlation = jnp.concatenate(pieces, axis=0)
    norm_sums = jnp.concatenate(norm_pieces, axis=0)
    energy = jnp.dot(counting, window, precision=lax.Precision.HIGHEST)
    denominator = energy * norm_sums[:, None] + epsilon
    return correlation * lax.rsqrt(denominator) * scale_factor


def only(condition, action):
    if condition is None:
        action()
        return

    @pl.when(condition)
    def _():
        action()


UP, DOWN, ACROSS, PLANE = range(4)


def kernel(
    tm,
    listing, traces, templates, out,
    T, X, W, S, CP, CC, CN, RC, RN, RP, E, WIN, EN, PA, PB,
    t_sem, x_sem, slab_sem, send_sem, recv_sem, tail_send, tail_recv,
):
    nblocks, depth, lags = traces.shape
    local_taps, members, rows = templates.shape
    listed = listing.shape[0]
    taps = local_taps * tm
    half = members // 2
    pair_taps = 2 * local_taps
    line = tm // 4
    chips = tm // 2
    shared = (3 * half // 4) // 2
    scale = math.sqrt(taps * rows)

    me = lax.axis_index("tm")
    plane = lax.axis_index("span")
    core = lax.rem(me, 2)
    chip = me // 2
    x = lax.rem(chip, 2)
    z = chip // 2

    def device(z_, x_, c_):
        return {"tm": (z_ * 2 + x_) * 2 + c_}

    sibling = device(z, x, 1 - core)
    targets = {
        UP: device(z + 1, x, core),
        DOWN: device(z - 1, x, core),
        ACROSS: device(z, 1 - x, core),
        PLANE: {"span": 1 - plane},
    }
    has_up, has_down = z + 1 < line, z > 0
    has_next, has_prev = chip + 1 < chips, chip > 0

    own_templates = pltpu.make_async_copy(templates, T, t_sem)
    own_templates.start()

    barrier = pltpu.get_barrier_semaphore()

    def greet(target):
        pl.semaphore_signal(barrier, inc=1, device_id=target, device_id_type=MESH)

    greet(sibling)
    greet(targets[ACROSS])
    greet(targets[PLANE])
    only(has_up, lambda: greet(targets[UP]))
    only(has_down, lambda: greet(targets[DOWN]))

    @pl.when(jnp.logical_and(has_next, core == 1))
    def _():
        greet({"tm": 2 * chip + 2})
        greet({"tm": 2 * chip + 3})

    own_traces = pltpu.make_async_copy(traces, X.at[core], x_sem.at[0])
    own_traces.start()
    own_templates.wait()
    S[...] = jnp.swapaxes(T[...], 0, 1)
    slab_rows = pl.ds(pl.multiple_of(me * local_taps, local_taps), local_taps)
    own_slab = pltpu.make_async_copy(
        S.at[pl.ds(core * half, half)], W.at[:, slab_rows, :], slab_sem.at[0]
    )
    own_slab.start()

    greetings = 3 + has_up.astype(jnp.int32) + has_down.astype(jnp.int32) + has_prev.astype(jnp.int32)
    pl.semaphore_wait(barrier, greetings)

    def remote(src, dst, send, recv, target):
        return pltpu.make_async_remote_copy(
            src_ref=src, dst_ref=dst, send_sem=send, recv_sem=recv,
            device_id=target, device_id_type=MESH,
        )

    other_slab = remote(
        S.at[pl.ds((1 - core) * half, half)], W.at[:, slab_rows, :],
        slab_sem.at[1], slab_sem.at[2], sibling,
    )
    other_slab.start()
    other_traces = [
        remote(traces.at[b], X.at[core, b], x_sem.at[1 + b], x_sem.at[1 + nblocks + b], sibling)
        for b in range(nblocks)
    ]

    def share(k):
        for b in range(k * nblocks // line, (k + 1) * nblocks // line):
            other_traces[b].start()


    started = []

    def move(way, j, p):
        part = W.at[j, pl.ds(pl.multiple_of(p * pair_taps, pair_taps), pair_taps), :]
        return remote(part, part, send_sem.at[way, j, p], recv_sem.at[j, p], targets[way])

    def send(way, j, p, allowed):
        started.append((way, j, p, allowed))
        only(allowed, lambda: move(way, j, p).start())

    def arrived(j, p, allowed):
        only(allowed, lambda: move(ACROSS, j, p).wait_recv())

    own_slab.wait()
    other_slab.wait_recv()

    mine = [plane * shared + i for i in range(shared)]
    theirs = [(1 - plane) * shared + i for i in range(shared)]
    both = list(range(2 * shared, half))
    flows = [(j, True) for j in mine] + [(j, False) for j in both]
    always = None

    def stage(flow, k):
        j, passed_on = flow
        here = lambda d: (z + d) * 2 + x
        there = lambda d: (z + d) * 2 + 1 - x
        if k == 0:
            send(UP, j, here(0), has_up)
            send(DOWN, j, here(0), has_down)
            send(ACROSS, j, here(0), always)
            return
        if k < line:
            below, above = z >= k, z + k < line
            arrived(j, here(-k), below)
            send(UP, j, here(-k), jnp.logical_and(below, has_up))
            send(ACROSS, j, here(-k), below)
            if passed_on:
                send(PLANE, j, here(-k), below)
            arrived(j, here(k), above)
            send(DOWN, j, here(k), jnp.logical_and(above, has_down))
            send(ACROSS, j, here(k), above)
            if passed_on:
                send(PLANE, j, here(k), above)
        d = k - 1
        if d == 0:
            arrived(j, there(0), always)
            if passed_on:
                send(PLANE, j, there(0), always)
        else:
            below, above = z >= d, z + d < line
            arrived(j, there(-d), below)
            if passed_on:
                send(PLANE, j, there(-d), below)
            arrived(j, there(d), above)
            if passed_on:
                send(PLANE, j, there(d), above)

    def passed(j):
        for d in range(1, chips):
            arrived(j, lax.rem(chip + d, chips), always)

    tile = 256
    half_taps = taps // 2
    pieces = lags // tile
    bands = half_taps // 8 // pieces
    unit = {"count": 0, "open": None, "partial": []}

    def multiply(j, h, n, slot):
        names = [listing[m, core * half + j] for m in range(listed)]
        chosen = jnp.concatenate([X[h, b, :, pl.ds(n * tile, tile)] for b in names], axis=0)
        slot[:, pl.ds(n * tile, tile)] = jnp.dot(W[j], chosen, preferred_element_type=jnp.float32)

    def shear(n, slot, total):
        for band in range(n * bands, (n + 1) * bands):
            row = 8 * band
            near = slot[pl.ds(row, 8), :]
            far = slot[pl.ds(row + half_taps, 8), :]
            gap = jnp.zeros((8, half_taps), jnp.float32)
            joined = jnp.concatenate([far, gap], axis=1) + jnp.concatenate([gap, near], axis=1)
            joined = jnp.concatenate([gap, joined], axis=1)
            if row:
                joined = pltpu.roll(joined, joined.shape[1] - row, 1)
            total = joined if total is None else total + joined
        return total

    def store(j):
        gap = jnp.zeros((8, lags), jnp.float32)
        low, high = unit["partial"]
        unit["partial"] = []
        sheared = jnp.concatenate([low, gap], axis=1) + jnp.concatenate([gap, high], axis=1)
        row_index = lax.broadcasted_iota(jnp.int32, sheared.shape, 0)
        for bit in (1, 2, 4):
            moved = pltpu.roll(sheared, sheared.shape[1] - bit, 1)
            sheared = jnp.where(lax.rem(row_index // bit, 2) == 1, moved, sheared)
        line_sum = jnp.sum(sheared, axis=0, keepdims=True)
        CP[pl.ds(j, 1), :] = line_sum[:, :taps]
        CC[0, pl.ds(j, 1), :] = line_sum[:, taps : taps + lags]
        CC[1, pl.ds(j, 1), :] = line_sum[:, taps + lags :]

    def advance(new):
        old = unit["open"]
        slots = (PA, PB) if unit["count"] % 2 == 0 else (PB, PA)
        total = None
        for n in range(pieces):
            if new is not None:
                multiply(*new, n, slots[0])
            if old is not None:
                total = shear(n, slots[1], total)
        if old is not None:
            unit["partial"].append(total)
            if old[1] == 1:
                store(old[0])
        unit["open"] = new
        unit["count"] += 1

    def correlate(j):
        advance((j, 0))
        wide = W[j].astype(jnp.float32)
        norm = jnp.sum(jnp.sum(wide * wide, axis=0, keepdims=True), axis=1, keepdims=True)
        CN[pl.ds(j, 1), :] = jnp.broadcast_to(norm, (1, CN.shape[1]))
        advance((j, 1))

    edge_send = remote(
        E.at[:, pl.ds(0, taps)], E.at[:, pl.ds(lags, taps)],
        tail_send.at[0], tail_recv.at[0], {"tm": me - 1},
    )

    def energies():
        own_traces.wait()
        for b in range(nblocks):
            part = X[core, b].astype(jnp.float32)
            E[pl.ds(b, 1), pl.ds(0, lags)] = jnp.sum(part * part, axis=0, keepdims=True)
        only(me > 0, edge_send.start)

        @pl.when(me + 1 == tm)
        def _():
            E[:, pl.ds(lags, taps)] = jnp.zeros((nblocks, taps), jnp.float32)

    def windows():
        only(me + 1 < tm, edge_send.wait_recv)
        window = E[...]
        reach = 1
        while reach < taps:
            window = window + pltpu.roll(window, window.shape[1] - reach, 1)
            reach *= 2
        for b in range(nblocks):
            WIN[b] = window[b : b + 1, :lags]
        for j in range(members):
            energy = WIN[listing[0, j]]
            for m in range(1, listed):
                energy = energy + WIN[listing[m, j]]
            EN[pl.ds(j, 1), :] = energy

    first, second = flows[:shared], flows[shared:]

    def stages(group, k):
        for flow in group:
            stage(flow, k)

    stages(first, 0)
    stages(second, 0)
    share(0)
    energies()
    for k in range(1, line):
        stages(first, k)
        if k < line - 1:
            stages(second, k)
        share(k)
    stages(first, line)
    for copy in other_traces:
        copy.wait_recv()
    for i, flow in enumerate(first):
        correlate(flow[0])
        if i == 0:
            stages(second, line - 1)
    stages(second, line)
    for flow in second:
        correlate(flow[0])
    windows()
    for j in theirs:
        passed(j)
        correlate(j)
    advance(None)

    mate = remote(CC.at[1 - core], RC, tail_send.at[1], tail_recv.at[1], sibling)
    norms = remote(CN, RN, tail_send.at[2], tail_recv.at[2], sibling)
    before = remote(
        CP, RP.at[core], tail_send.at[3], tail_recv.at[3 + core], {"tm": 2 * chip - 1}
    )
    mate.start()
    norms.start()
    only(has_prev, before.start)
    mate.wait_recv()
    norms.wait_recv()

    mine_rows = pl.ds(pl.multiple_of(core * half, half), half)
    mate_rows = pl.ds(pl.multiple_of((1 - core) * half, half), half)

    takes = jnp.logical_and(has_next, core == 1)

    @pl.when(takes)
    def _():
        for c in range(2):
            remote(CP, RP.at[c], tail_send.at[3], tail_recv.at[3 + c], sibling).wait_recv()

    def finish(value, rows_, norm, tail):
        denominator = EN[rows_, :] * norm[:, :1] + epsilon
        factor = lax.rsqrt(denominator) * scale
        out[rows_, :] = value * factor

        @pl.when(takes)
        def _():
            last = pl.ds(lags - taps, taps)
            out[rows_, last] = (value[:, lags - taps :] + tail()) * factor[:, lags - taps :]

    finish(CC[core], mine_rows, CN[...], lambda: RP[core])
    finish(RC[...], mate_rows, RN[...], lambda: RP[1 - core])

    other_slab.wait_send()
    for copy in other_traces:
        copy.wait_send()
    mate.wait_send()
    norms.wait_send()
    only(has_prev, before.wait_send)
    only(me > 0, edge_send.wait_send)
    for way, j, p, allowed in started:
        only(allowed, move(way, j, p).wait_send)


def fused(traces, templates, blocks):
    channels, lags = traces.shape
    local_taps, members, rows = templates.shape
    tm = lax.axis_size("tm")
    taps = local_taps * tm
    half = members // 2
    depth = rows // blocks.shape[1]
    nblocks = channels // depth
    chips = tm // 2
    vmem = pl.BlockSpec(memory_space=pltpu.VMEM)
    f32 = jnp.float32
    return pl.pallas_call(
        functools.partial(kernel, tm),
        out_shape=jax.ShapeDtypeStruct((members, lags), f32),
        in_specs=[
            pl.BlockSpec(memory_space=pltpu.SMEM),
            pl.BlockSpec(memory_space=pl.ANY),
            pl.BlockSpec(memory_space=pl.ANY),
        ],
        out_specs=vmem,
        scratch_shapes=[
            pltpu.VMEM(templates.shape, templates.dtype),
            pltpu.VMEM((2, nblocks, depth, lags), traces.dtype),
            pltpu.VMEM((half, taps, rows), templates.dtype),
            pltpu.VMEM((members, local_taps, rows), templates.dtype),
            pltpu.VMEM((half, taps), f32),
            pltpu.VMEM((2, half, lags), f32),
            pltpu.VMEM((half, 128), f32),
            pltpu.VMEM((half, lags), f32),
            pltpu.VMEM((half, 128), f32),
            pltpu.VMEM((2, half, taps), f32),
            pltpu.VMEM((nblocks, lags + taps), f32),
            pltpu.VMEM((nblocks, 1, lags), f32),
            pltpu.VMEM((members, lags), f32),
            pltpu.VMEM((taps, lags), f32),
            pltpu.VMEM((taps, lags), f32),
            pltpu.SemaphoreType.DMA,
            pltpu.SemaphoreType.DMA((1 + 2 * nblocks,)),
            pltpu.SemaphoreType.DMA((3,)),
            pltpu.SemaphoreType.DMA((4, half, chips)),
            pltpu.SemaphoreType.DMA((half, chips)),
            pltpu.SemaphoreType.DMA((4,)),
            pltpu.SemaphoreType.DMA((5,)),
        ],
        compiler_params=pltpu.CompilerParams(
            collective_id=0, has_side_effects=True, vmem_limit_bytes=60 * 2**20
        ),
    )(blocks.T, traces.reshape(nblocks, depth, lags), templates)


def per_device(traces, templates, blocks):
    channels, lags = traces.shape
    local_taps, members, rows = templates.shape
    tm = lax.axis_size("tm")
    taps = local_taps * tm
    fits = (
        lax.axis_size("span") == 2
        and tm % 4 == 0
        and local_taps % 16 == 0
        and members == 16
        and taps == 256
        and lags % 256 == 0
        and (taps // 16) % (lags // 256) == 0
        and rows % (128 * blocks.shape[1]) == 0
    )
    return (fused if fits else plain)(traces, templates, blocks)


def solution(mesh):
    return jax.shard_map(
        per_device,
        mesh=mesh,
        in_specs=(P(None, ("span", "tm")), P("tm", None, None), P()),
        out_specs=P(None, ("span", "tm")),
        check_vma=False,
    )
```
